32 devices in a mesh: grp: 4 (over y, core), tok: 8 (over z, x).
Axes of the slice: x: 2, y: 2, z: 4, core: 2. Of those that a mesh axis runs over, the one named last changes fastest.
Arguments:
- pre_q: bfloat16 [2048, 4096], P(('grp', 'tok')), may hold values from -64 to 64
- pre_kv: bfloat16 [2048, 2048], P(('grp', 'tok')), may hold values from -8 to 8
- pre_segment: int32 [4, 512], P('grp'), may hold values from 0 to 1, never falling along the last dimension, each value on 1 to 384 neighbouring positions
- dec_q: bfloat16 [32, 4096], P(('grp', 'tok')), may hold values from -64 to 64
- cache: bfloat16 [32, 512, 2048], P(('grp', 'tok')), may hold values from -8 to 8
- cache_len: int32 [32], P(('grp', 'tok')), may hold values from 1 to 512, 8192 in all
- slot_request: int32 [32], replicated, may hold values from 0 to 31, each once
- resid: bfloat16 [2080, 4096], P('grp', 'tok'), may hold values from -64 to 64
- wo: bfloat16 [4096, 4096], P(None, 'tok'), may hold values from -0.5 to 0.5
- tenant: int32 [4, 520], P('grp'), may hold values from 0 to 3, never falling along the last dimension, each value on 1 to 260 neighbouring positions
- norm_gain: float32 [4, 4096], replicated, may hold values from 0.25 to 1.75
- w_gate: bfloat16 [4096, 12288], P(None, 'tok'), may hold values from -0.09375 to 0.09375
- w_up: bfloat16 [4096, 12288], P(None, 'tok'), may hold values from -0.09375 to 0.09375
- w_down: bfloat16 [12288, 4096], P('tok'), may hold values from -0.0546875 to 0.0546875
Outputs:
- out: bfloat16 [2080, 4096], P('grp', 'tok')
The draws below stay inside these ranges and needn't reach their ends.
All inputs are finite; a program needn't handle non-finite values. No bound on the sum of `cache_len` on one device may be relied on, other than what follows from the above.
Results may differ from the reference program's by a relative error of at most 0.011.
Values may be sent and summed in bfloat16 or wider, within the bound.
No kernel may reach another device: no remote copies, remote signals or barrier semaphores. Data moves between devices by JAX's collectives and lax.ppermute only.
A program may use at most 128 MiB of HBM per device.

```python
import math
import jax
import jax.numpy as jnp
import numpy as np
from jax import lax

D = 4096
H = 32
KVH = 8
HD = 128
FFW = 12288
TENANTS = 4
PRE_DEV = 64
CMAX = 512
PB = 512
GT = 520
TOKENS = 2080
PRE = 2048
DEC = 32
SEG_CNT = 2
SEG_MOST = 384
N_GRP = 4
N_TOK = 8


def prefill_pair(key):
    query_key = jax.random.fold_in(key, 101)
    pair_key = jax.random.fold_in(key, 102)
    width = KVH * HD
    queries = jnp.clip(jax.random.normal(query_key, (PRE, D), jnp.float32), -6.0, 6.0)
    pairs = jnp.clip(jax.random.normal(pair_key, (PRE, 2 * width), jnp.float32), -6.0, 6.0)
    return (queries, pairs)


def draw_pre_q(key, part):
    return prefill_pair(key)[0].astype(jnp.bfloat16)


def draw_pre_kv(key, part):
    return prefill_pair(key)[1].astype(jnp.bfloat16)


def decode_pair(key):
    query_key = jax.random.fold_in(key, 201)
    cache_key = jax.random.fold_in(key, 202)
    width = KVH * HD
    queries = jnp.clip(jax.random.normal(query_key, (DEC, D), jnp.float32), -6.0, 6.0)
    entries = jnp.clip(jax.random.normal(cache_key, (DEC, CMAX, 2 * width), jnp.float32), -6.0, 6.0)
    return (queries, entries)


def draw_dec_q(key, part):
    return decode_pair(key)[0].astype(jnp.bfloat16)


def draw_cache(key, part):
    return decode_pair(key)[1].astype(jnp.bfloat16)


def draw_resid(key, part):
    base_key = jax.random.fold_in(key, 301)
    row_key = jax.random.fold_in(key, 302)
    column_key = jax.random.fold_in(key, 303)
    base = jnp.clip(jax.random.normal(base_key, (TOKENS, D), jnp.float32), -6.0, 6.0)
    row_scale = jnp.exp(jax.random.uniform(row_key, (TOKENS, 1), jnp.float32, 0.0, math.log(10.0)))
    rising = math.log(3.0) * jnp.arange(D).astype(jnp.float32)[None, :] / D
    column_scale = jnp.exp(jax.random.uniform(column_key, (1, D), jnp.float32, 0.0, math.log(4.0)) + rising)
    return (0.08 * base * row_scale * column_scale).astype(jnp.bfloat16)


def level_of(stream_key, extent, pieces, least, high):
    def one(axis_at, blocks):
        heights = jax.random.uniform(jax.random.fold_in(jax.random.fold_in(stream_key, 6), axis_at), (blocks,), jnp.float32, least / len(pieces), high / len(pieces))
        return jnp.repeat(jnp.exp(heights), extent[axis_at] // blocks).reshape((-1,) + (1,) * (len(extent) - axis_at - 1))

    loudness = one(*pieces[0])
    for cut in pieces[1:]:
        loudness = loudness * one(*cut)
    return loudness


def profile(amount, total, most, skew):
    loads = [(1 << 20) // math.isqrt(standing ** skew) + 1 for standing in range(2, amount + 1)]
    rest, counts = total - most - (amount - 1), [1] * (amount - 1)
    while rest > 0:
        free = [i for i in range(amount - 1) if counts[i] < most]
        whole, left = sum([loads[i] for i in free]), rest
        for i in free:
            more = min(most - counts[i], max(1, left * loads[i] // whole), rest)
            counts[i] = counts[i] + more
            rest = rest - more
    return np.array([most] + counts)


def uneven_parts(stream_key, amount, total, limit, skew):
    if amount == 2:
        one = jax.random.randint(stream_key, (), max(1, total - limit), min(limit, total - 1) + 1)
        return jnp.stack([one, total - one])
    sizes = jnp.asarray(profile(amount, total, limit, skew), jnp.int32)
    couples = (amount - 1) // 2
    source_of, taker = sizes[1:1 + 2 * couples:2], sizes[2:2 + 2 * couples:2]
    slack = jnp.minimum(source_of - 1, limit - taker)
    passed = jax.random.randint(jax.random.fold_in(stream_key, 1), (couples,), 0, 1 << 20) % (slack + 1)
    sizes = sizes.at[1:1 + 2 * couples:2].set(source_of - passed).at[2:2 + 2 * couples:2].set(taker + passed)
    return sizes[jax.random.permutation(jax.random.fold_in(stream_key, 2), amount)]


def noise(own_key, dims, spread, most, split=(), held_as=jnp.bfloat16):
    values = jax.random.normal(own_key, dims, jnp.float32) * spread
    if len(split) > 0:
        values = level_of(own_key, dims, split, -0.22, 0.18) * values
    return jnp.clip(values, min=-most, max=most).astype(held_as)


def setup_inputs(seed: int = 0) -> dict:
    arg_keys = jax.random.split(jax.random.key(seed), 15)
    pre_q = draw_pre_q(jax.random.fold_in(arg_keys[14], 71), 0)
    pre_kv = draw_pre_kv(jax.random.fold_in(arg_keys[14], 71), 0)
    pre_segment = jax.vmap(lambda own: jnp.searchsorted(jnp.cumsum(uneven_parts(own, SEG_CNT, PB, SEG_MOST, 0)), jnp.arange(PB), side="right"))(jax.random.split(arg_keys[2], N_GRP)).reshape((N_GRP, PB)).astype(jnp.int32)
    dec_q = draw_dec_q(jax.random.fold_in(arg_keys[14], 71), 0)
    cache = draw_cache(jax.random.fold_in(arg_keys[14], 71), 0)
    cache_len = uneven_parts(arg_keys[5], DEC, DEC * CMAX // 2, CMAX, 2).astype(jnp.int32)
    slot_request = jax.random.permutation(arg_keys[6], DEC).astype(jnp.int32)
    resid = draw_resid(jax.random.fold_in(arg_keys[14], 71), 0)
    wo = noise(arg_keys[8], (D, D), HD ** -0.5, 0.5, ((1, 8),))
    tenant = jax.vmap(lambda own: jnp.searchsorted(jnp.cumsum(uneven_parts(own, TENANTS, GT, GT // 2, 0)), jnp.arange(GT), side="right"))(jax.random.split(arg_keys[9], N_GRP)).reshape((N_GRP, GT)).astype(jnp.int32)
    norm_gain = jnp.clip(1.0 + 0.15 * jax.random.normal(arg_keys[10], (TENANTS, D), jnp.float32), 0.25, 1.75)
    w_gate = noise(arg_keys[11], (D, FFW), D ** -0.5, 0.09375, ((1, 8),))
    w_up = noise(arg_keys[12], (D, FFW), D ** -0.5, 0.09375, ((1, 8),))
    w_down = noise(arg_keys[13], (FFW, D), FFW ** -0.5, 0.0546875, ((0, 8),))
    return {"pre_q": pre_q, "pre_kv": pre_kv, "pre_segment": pre_segment, "dec_q": dec_q, "cache": cache, "cache_len": cache_len, "slot_request": slot_request, "resid": resid, "wo": wo, "tenant": tenant, "norm_gain": norm_gain, "w_gate": w_gate, "w_up": w_up, "w_down": w_down}


epsilon = 1e-05

def prefill_group(inputs):
    queries, pairs, segment = inputs
    group = H // KVH
    positions = jnp.arange(PB)
    allowed = (positions[None, :] <= positions[:, None]) & (segment[None, :] == segment[:, None])
    queries = queries.reshape(PB, KVH, group, HD).transpose(1, 0, 2, 3).astype(jnp.float32)
    keys = pairs[:, :KVH * HD].reshape(PB, KVH, HD).transpose(1, 0, 2).astype(jnp.float32)
    values = pairs[:, KVH * HD:].reshape(PB, KVH, HD).transpose(1, 0, 2).astype(jnp.float32)

    def one_head(head_inputs):
        query_head, key_head, value_head = head_inputs
        scores = jnp.einsum('qgd,nd->gqn', query_head, key_head) / math.sqrt(HD)
        masked = jnp.where(allowed[None], scores, -jnp.inf)
        highest = lax.optimization_barrier(jnp.max(masked, axis=-1, keepdims=True))
        weights = jnp.exp(masked - highest).astype(jnp.bfloat16)
        weights = lax.optimization_barrier(weights).astype(jnp.float32)
        totals = lax.optimization_barrier(jnp.sum(weights, axis=-1))
        mixed = jnp.einsum('gqn,nd->gqd', weights, value_head)
        return mixed / totals[..., None]
    heads_out = lax.map(one_head, (queries, keys, values))
    return heads_out.transpose(2, 0, 1, 3).reshape(PB, D).astype(jnp.bfloat16)

def decode_slot(inputs):
    query, entries, length = inputs
    group = H // KVH
    query = query.reshape(KVH, group, HD).astype(jnp.float32)
    keys = entries[:, :KVH * HD].reshape(CMAX, KVH, HD).astype(jnp.float32)
    values = entries[:, KVH * HD:].reshape(CMAX, KVH, HD).astype(jnp.float32)
    scores = jnp.einsum('kgd,pkd->kgp', query, keys) / math.sqrt(HD)
    visible = jnp.arange(CMAX) < length
    masked = jnp.where(visible, scores, -jnp.inf)
    highest = lax.optimization_barrier(jnp.max(masked, axis=-1, keepdims=True))
    weights = jnp.exp(masked - highest).astype(jnp.bfloat16)
    weights = lax.optimization_barrier(weights).astype(jnp.float32)
    totals = lax.optimization_barrier(jnp.sum(weights, axis=-1))
    mixed = jnp.einsum('kgp,pkd->kgd', weights, values)
    return (mixed / totals[..., None]).reshape(D).astype(jnp.bfloat16)

def reference(pre_q, pre_kv, pre_segment, dec_q, cache, cache_len, slot_request, resid, wo, tenant, norm_gain, w_gate, w_up, w_down):
    prefill_att = lax.map(prefill_group, (pre_q.reshape(N_GRP, PB, D), pre_kv.reshape(N_GRP, PB, 2 * KVH * HD), pre_segment))
    prefill_att = prefill_att.reshape(N_GRP, N_TOK, PRE_DEV, D)
    slot_queries = dec_q[slot_request.astype(jnp.int32)]
    decode_att = lax.map(decode_slot, (slot_queries, cache, cache_len)).reshape(N_GRP, N_TOK, 1, D)
    attention = jnp.concatenate([prefill_att, decode_att], axis=2).reshape(TOKENS, D)
    mixed_in = (resid.astype(jnp.float32) + jnp.dot(attention, wo, preferred_element_type=jnp.float32)).astype(jnp.bfloat16)

    def feed_group(inputs):
        rows_in, owners = inputs
        wide = rows_in.astype(jnp.float32)
        mean_square = lax.optimization_barrier(jnp.mean(wide * wide, axis=-1, keepdims=True))
        one_hot = (owners[:, None] == jnp.arange(TENANTS)[None, :]).astype(jnp.float32)
        gains = jnp.dot(one_hot, norm_gain, precision=lax.Precision.HIGHEST)
        normed = (wide * lax.rsqrt(mean_square + epsilon) * gains).astype(jnp.bfloat16)
        gate_part = jnp.dot(normed, w_gate, preferred_element_type=jnp.float32)
        lift_part = jnp.dot(normed, w_up, preferred_element_type=jnp.float32)
        hidden = (jax.nn.silu(gate_part) * lift_part).astype(jnp.bfloat16)
        return (wide + jnp.dot(hidden, w_down, preferred_element_type=jnp.float32)).astype(jnp.bfloat16)
    result = lax.map(feed_group, (mixed_in.reshape(N_GRP, GT, D), tenant))
    return result.reshape(TOKENS, D)
```

```python
import functools
import math

import jax
import jax.numpy as jnp
from jax import lax
from jax.experimental import pallas as pl
from jax.experimental.pallas import tpu as pltpu
from jax.sharding import PartitionSpec as P

D = 4096
H = 32
KVH = 8
HD = 128
GROUP = H // KVH
WIDTH = KVH * HD
EPS = 1e-05
NEG = -1e30
Z_CHIPS = 4

ANY = pl.BlockSpec(memory_space=pl.ANY)
VMEM = pl.BlockSpec(memory_space=pltpu.VMEM)
SMEM = pl.BlockSpec(memory_space=pltpu.SMEM)
F32 = jnp.float32
BF16 = jnp.bfloat16


def ring_order(n):
    columns = n // Z_CHIPS
    if n % Z_CHIPS or columns % 2:
        return list(range(n))
    order = [z * columns for z in range(Z_CHIPS)]
    for i, z in enumerate(reversed(range(Z_CHIPS))):
        xs = range(1, columns) if i % 2 == 0 else range(columns - 1, 0, -1)
        order += [z * columns + x for x in xs]
    return order


def params(mib):
    return pltpu.CompilerParams(vmem_limit_bytes=mib * 2**20)


def cost(flops, moved, exps=0):
    return pl.CostEstimate(flops=int(flops), bytes_accessed=int(moved), transcendentals=int(exps))


def copies(pairs, sems):
    out = [pltpu.make_async_copy(src, dst, sems.at[i]) for i, (src, dst) in enumerate(pairs)]
    for c in out:
        c.start()
    return out


def row_parts(parts, owners, target, rows):
    n = len(parts) - 1
    half = n // 2
    pairs = []
    for i, part in enumerate(parts):
        d = i if i <= half else i - 1
        start = owners[d] * rows
        if i == half:
            pairs.append((part, target.at[pl.ds(pl.multiple_of(start, 16), rows // 2)]))
        elif i == half + 1:
            pairs.append((part, target.at[pl.ds(pl.multiple_of(start + rows // 2, 16), rows // 2)]))
        else:
            pairs.append((part, target.at[pl.ds(pl.multiple_of(start, 16), rows)]))
    return pairs


def attention_kernel(n, first, rows, owners, here, q_ref, segcol_ref, seg_ref, *rest):
    parts, (out_ref, kv, sems) = rest[: n + 1], rest[n + 1 :]
    total = kv.shape[0]
    moving = copies(row_parts(parts, owners, kv, total // n), sems)
    key_pos = lax.broadcasted_iota(jnp.int32, (rows, total), 1)
    query_pos = lax.broadcasted_iota(jnp.int32, (rows, total), 0) + (here[0] + first)
    seen = (key_pos <= query_pos) & (segcol_ref[first : first + rows, :] == seg_ref[...])
    bias = jnp.where(seen, 0.0, NEG).astype(F32)
    bias = jnp.concatenate([bias] * GROUP, axis=0)
    for c in moving:
        c.wait()
    for k in range(KVH):
        q = jnp.concatenate(
            [q_ref[first : first + rows, (k * GROUP + g) * HD : (k * GROUP + g + 1) * HD] for g in range(GROUP)],
            axis=0,
        )
        s = lax.dot_general(
            q, kv[:, k * HD : (k + 1) * HD], (((1,), (1,)), ((), ())), preferred_element_type=F32
        )
        s = s * (1.0 / math.sqrt(HD)) + bias
        w = jnp.exp(s - jnp.max(s, axis=-1, keepdims=True)).astype(BF16)
        t = jnp.sum(w.astype(F32), axis=-1, keepdims=True)
        o = jnp.dot(w, kv[:, WIDTH + k * HD : WIDTH + (k + 1) * HD], preferred_element_type=F32) / t
        for g in range(GROUP):
            out_ref[:, (k * GROUP + g) * HD : (k * GROUP + g + 1) * HD] = o[g * rows : (g + 1) * rows].astype(BF16)


def attention(n, first, rows, owners, here, q, segcol, seg, parts):
    total = seg.shape[1]
    return pl.pallas_call(
        functools.partial(attention_kernel, n, first, rows),
        out_shape=jax.ShapeDtypeStruct((rows, D), BF16),
        in_specs=[SMEM, SMEM, VMEM, VMEM, VMEM] + [ANY] * (n + 1),
        out_specs=VMEM,
        scratch_shapes=[pltpu.VMEM((total, 2 * WIDTH), BF16), pltpu.SemaphoreType.DMA((n + 1,))],
        compiler_params=params(20),
        cost_estimate=cost(4 * rows * H * HD * total, 4 * total * WIDTH, rows * H * total),
        name="prefill_attention",
    )(owners, here, q, segcol, seg, *parts)


def decode_kernel(length, q_ref, cache_ref, out_ref):
    positions = cache_ref.shape[1]
    head = lax.broadcasted_iota(jnp.int32, (H, positions), 0) // GROUP
    q = q_ref[...]
    s = jnp.zeros((H, positions), F32)
    for k in range(KVH):
        one = lax.dot_general(
            q, cache_ref[0, :, k * HD : (k + 1) * HD], (((1,), (1,)), ((), ())), preferred_element_type=F32
        )
        s = jnp.where(head == k, one, s)
    spot = lax.broadcasted_iota(jnp.int32, (H, positions), 1)
    s = jnp.where(spot < length[0], s * (1.0 / math.sqrt(HD)), NEG)
    w = jnp.exp(s - jnp.max(s, axis=-1, keepdims=True)).astype(BF16).astype(F32)
    t = jnp.sum(w, axis=-1, keepdims=True)
    o = jnp.zeros((H, HD), F32)
    for k in range(KVH):
        mine = jnp.where(head == k, w, 0.0).astype(BF16)
        o = o + jnp.dot(
            mine, cache_ref[0, :, WIDTH + k * HD : WIDTH + (k + 1) * HD], preferred_element_type=F32
        )
    out_ref[...] = (o / t).astype(BF16)


def decode(length, q, cache):
    return pl.pallas_call(
        decode_kernel,
        out_shape=jax.ShapeDtypeStruct((H, HD), BF16),
        in_specs=[SMEM, VMEM, VMEM],
        out_specs=VMEM,
        compiler_params=params(20),
        cost_estimate=cost(4 * H * WIDTH * cache.shape[1], 2 * cache.size, H * cache.shape[1]),
        name="decode_attention",
    )(length, q, cache)


def project_kernel(n, rows, extra, owners, *rest):
    if extra:
        dec_ref, perm_ref, rest = rest[0], rest[1], rest[2:]
    parts, (wo_ref, resid_ref, out_ref, x, w, sems, wsems) = rest[: n + 1], rest[n + 1 :]
    moving = copies(row_parts(parts, owners, x, rows), sems)
    steps = 4
    deep = D // steps
    slabs = [pl.ds(i * deep, deep) for i in range(steps)]
    weights = copies([(wo_ref.at[s], w.at[s]) for s in slabs], wsems)
    if extra:
        x[n * rows :, :] = jnp.dot(perm_ref[...], dec_ref[...], preferred_element_type=F32).astype(BF16)
    for c in moving:
        c.wait()
    total = resid_ref[...].astype(F32)
    for i in range(steps):
        weights[i].wait()
        cut = slice(i * deep, (i + 1) * deep)
        total = total + jnp.dot(x[:, cut], w[cut, :], preferred_element_type=F32)
    out_ref[...] = total.astype(BF16)


def project(n, rows, owners, parts, wo, resid, dec=None, perm=None):
    m, cols = resid.shape
    extra = dec is not None
    return pl.pallas_call(
        functools.partial(project_kernel, n, rows, extra),
        out_shape=jax.ShapeDtypeStruct((m, cols), BF16),
        in_specs=[SMEM] + [VMEM] * (2 * extra) + [ANY] * (n + 2) + [VMEM],
        out_specs=VMEM,
        scratch_shapes=[
            pltpu.VMEM((m, D), BF16),
            pltpu.VMEM((D, cols), BF16),
            pltpu.SemaphoreType.DMA((n + 1,)),
            pltpu.SemaphoreType.DMA((4,)),
        ],
        compiler_params=params(20),
        cost_estimate=cost(2 * m * D * cols, 2 * D * (m + cols)),
        name="out_projection",
    )(owners, *([dec, perm] if extra else []), *parts, wo, resid)


def norm_kernel(n, cut, owners, tenants_ref, gain_ref, *rest):
    parts, (out_ref, x, sems) = rest[: n + 1], rest[n + 1 :]
    m = x.shape[0]
    cols = D // n
    half = n // 2
    pairs = []
    for i, part in enumerate(parts):
        d = i if i <= half else i - 1
        at = pl.ds(pl.multiple_of(owners[d] * cols, 128), cols)
        if i == half:
            pairs.append((part, x.at[pl.ds(0, cut), at]))
        elif i == half + 1:
            pairs.append((part, x.at[pl.ds(cut, m - cut), at]))
        else:
            pairs.append((part, x.at[:, at]))
    for c in copies(pairs, sems):
        c.wait()
    square = jnp.zeros((m, 1), F32)
    for j in range(n):
        wide = x[:, j * cols : (j + 1) * cols].astype(F32)
        square = square + jnp.sum(wide * wide, axis=-1, keepdims=True)
    scale = lax.rsqrt(square / D + EPS)
    tenants = tenants_ref[...]
    for j in range(n):
        at = slice(j * cols, (j + 1) * cols)
        gain = jnp.broadcast_to(gain_ref[0:1, at], (m, cols))
        for t in range(1, gain_ref.shape[0]):
            gain = jnp.where(tenants == t, gain_ref[t : t + 1, at], gain)
        out_ref[:, at] = (x[:, at].astype(F32) * scale * gain).astype(BF16)


def normalize(n, cut, owners, tenants, gain, parts):
    m = tenants.shape[0]
    return pl.pallas_call(
        functools.partial(norm_kernel, n, cut),
        out_shape=jax.ShapeDtypeStruct((m, D), BF16),
        in_specs=[SMEM, VMEM, VMEM] + [ANY] * (n + 1),
        out_specs=VMEM,
        scratch_shapes=[pltpu.VMEM((m, D), BF16), pltpu.SemaphoreType.DMA((n + 1,))],
        compiler_params=params(20),
        cost_estimate=cost(12 * m * D, 4 * m * D),
        name="tenant_norm",
    )(owners, tenants, gain, *parts)


def swiglu_kernel(x_ref, gate_ref, up_ref, out_ref):
    x = x_ref[...]
    gate = jnp.dot(x, gate_ref[...], preferred_element_type=F32)
    lift = jnp.dot(x, up_ref[...], preferred_element_type=F32)
    out_ref[...] = (gate / (1.0 + jnp.exp(-gate)) * lift).astype(BF16)


def swiglu(x, w_gate, w_up, first, count, tile):
    m = x.shape[0]
    weight = pl.BlockSpec((D, tile), lambda i: (0, first + i))
    return pl.pallas_call(
        swiglu_kernel,
        out_shape=jax.ShapeDtypeStruct((m, count * tile), BF16),
        grid=(count,),
        in_specs=[pl.BlockSpec((m, D), lambda i: (0, 0)), weight, weight],
        out_specs=pl.BlockSpec((m, tile), lambda i: (0, i)),
        compiler_params=params(24),
        cost_estimate=cost(4 * m * D * count * tile, 4 * D * count * tile + 2 * m * D),
        name="gate_up",
    )(x, w_gate, w_up)


def down_kernel(stage, pieces, cut, blocks, *rest):
    hidden, rest = rest[:pieces], rest[pieces:]
    two = stage in ("second", "middle")
    got = 0 if stage == "first" else 2
    w_ref, rest = rest[0], rest[1:]
    arrived, rest = rest[:got], rest[got:]
    if stage == "last":
        own, rest = rest[0], rest[1:]
        outs, (w, sems) = rest[:1], rest[1:]
    else:
        outs, (w, sems) = rest[:2], rest[2:]
    cols = w.shape[-1]
    count = 2 if two else 1
    weights = copies(
        [
            (w_ref.at[:, pl.ds(pl.multiple_of(blocks[i] * cols, 128), cols)], w.at[i])
            for i in range(count)
        ],
        sems,
    )

    def block(i):
        weights[i].wait()
        total = None
        for j, h in enumerate(hidden):
            deep = h.shape[1]
            part = jnp.dot(h[...], w[i, j * deep : (j + 1) * deep, :], preferred_element_type=F32)
            total = part if total is None else total + part
        return total

    if stage == "first":
        total = block(0)
        outs[0][...] = total[:cut].astype(BF16)
        outs[1][...] = total[cut:].astype(BF16)
    elif stage == "second":
        total = block(0)
        outs[0][:cut] = (total[:cut] + arrived[0][...].astype(F32)).astype(BF16)
        outs[0][cut:] = total[cut:].astype(BF16)
        total = block(1)
        outs[1][:cut] = total[:cut].astype(BF16)
        outs[1][cut:] = (total[cut:] + arrived[1][...].astype(F32)).astype(BF16)
    elif stage == "middle":
        for i in range(2):
            outs[i][...] = (block(i) + arrived[i][...].astype(F32)).astype(BF16)
    else:
        total = block(0) + arrived[0][...].astype(F32) + arrived[1][...].astype(F32)
        outs[0][...] = (total + own[...].astype(F32)).astype(BF16)


def down(stage, cut, blocks, hidden, w_down, arrived, cols, own=None):
    m = hidden[0].shape[0]
    deep = w_down.shape[0]
    two = stage in ("second", "middle")
    if stage == "first":
        shapes = [(cut, cols), (m - cut, cols)]
    elif two:
        shapes = [(m, cols)] * 2
    else:
        shapes = [(m, cols)]
    given = list(arrived) + ([own] if stage == "last" else [])
    out = pl.pallas_call(
        functools.partial(down_kernel, stage, len(hidden), cut),
        out_shape=[jax.ShapeDtypeStruct(s, BF16) for s in shapes],
        in_specs=[SMEM] + [VMEM] * len(hidden) + [ANY] + [VMEM] * len(given),
        out_specs=[VMEM] * len(shapes),
        scratch_shapes=[pltpu.VMEM((1 + two, deep, cols), BF16), pltpu.SemaphoreType.DMA((1 + two,))],
        compiler_params=params(20),
        cost_estimate=cost(2 * m * deep * cols * (1 + two), 2 * (1 + two) * deep * cols),
        name="down_" + stage,
    )(blocks, *hidden, w_down, *given)
    return out


class Ring:
    def __init__(self, n, order, cut):
        self.n, self.half, self.cut = n, n // 2, cut
        self.fw = [(order[i], order[(i + 1) % n]) for i in range(n)]
        self.bw = [(b, a) for a, b in self.fw]

    def send(self, forward, backward):
        return lax.ppermute(forward, "tok", self.fw), lax.ppermute(backward, "tok", self.bw)

    def gather(self, own, whole_last=False):
        f = b = own
        ahead, behind = [], []
        for step in range(1, self.half):
            f, b = self.send(f, b)
            ahead.append(f)
            behind.append(b)
        if whole_last:
            last = [lax.ppermute(f, "tok", self.fw)]
        else:
            last = list(self.send(f[: self.cut], b[self.cut :]))
        return [own] + ahead + last + behind[::-1]


def shards(
    pre_q,
    pre_kv,
    pre_segment,
    dec_q,
    cache,
    cache_len,
    slot_request,
    resid,
    wo,
    tenant,
    norm_gain,
    w_gate,
    w_up,
    w_down,
):
    n, groups = lax.axis_size("tok"), lax.axis_size("grp")
    tok, grp = lax.axis_index("tok"), lax.axis_index("grp")
    local = pre_q.shape[0]
    rows = local // 2
    cols = wo.shape[1]
    order = ring_order(n)
    order_of = jnp.array(order, jnp.int32)
    place_of = jnp.array([order.index(i) for i in range(n)], jnp.int32)
    place = place_of[tok]
    owners = order_of[(place - jnp.arange(n, dtype=jnp.int32)) % n]
    here = jnp.reshape(tok * local, (1,)).astype(jnp.int32)

    parts = Ring(n, order, local // 2).gather(pre_kv)
    asked = jnp.concatenate(Ring(n, order, 0).gather(dec_q, whole_last=True), axis=0)
    choices = []
    for j in range(groups):
        request = slot_request[(grp ^ j) * n + tok]
        row = lax.dynamic_slice_in_dim(asked, (place - place_of[request % n]) % n, 1, 0)
        if j:
            row = lax.ppermute(row, "grp", [(g, g ^ j) for g in range(groups)])
        choices.append(row)
    mine = slot_request[grp * n + tok] // n
    query = lax.dynamic_slice_in_dim(jnp.concatenate(choices, axis=0), mine ^ grp, 1, 0)

    segcol = lax.dynamic_slice_in_dim(pre_segment, tok * local, local, 1).reshape(local, 1)
    spare = -(-n // 16) * 16
    own_att = [
        attention(n, c * rows, rows, owners, here, pre_q, segcol, pre_segment, parts) for c in range(2)
    ]
    own_dec = decode(cache_len, query.reshape(H, HD), cache).reshape(1, D)

    def split(a, fill):
        a = a.reshape(n, local + 1, -1)
        first = a[:, :rows].reshape(n * rows, -1)
        second = a[:, rows:local].reshape(n * rows, -1)
        tail = jnp.concatenate([a[:, local], jnp.full((spare - n, a.shape[-1]), fill, a.dtype)], axis=0)
        return first, jnp.concatenate([second, tail], axis=0)

    resids = split(resid, 0)
    tenants = split(tenant[0][:, None], 0)

    dec_parts = Ring(n, order, 0).gather(own_dec, whole_last=True)
    dec_all = jnp.concatenate(dec_parts + [jnp.zeros((spare - n, D), BF16)], axis=0)
    perm = (jnp.arange(spare)[:, None] == jnp.concatenate([owners, jnp.full((spare - n,), -1, jnp.int32)])[None, :])
    perm = perm.astype(BF16)

    results = []
    for c in range(2):
        ring = Ring(n, order, rows // 2)
        att = ring.gather(own_att[c])
        extra = (dec_all, perm) if c else ()
        mixed = project(n, rows, owners, att, wo, resids[c], *extra)
        m = mixed.shape[0]
        cut = (m // 32) * 16
        ring = Ring(n, order, cut)
        everywhere = ring.gather(mixed)
        normed = normalize(n, cut, owners, tenants[c], norm_gain, everywhere)
        tile = 256
        tiles = w_gate.shape[1] // tile
        per = 2
        hidden = [swiglu(normed, w_gate, w_up, i, min(per, tiles - i), tile) for i in range(0, tiles, per)]
        half = n // 2

        def target(d):
            return order_of[(place + d) % n]

        sent = down("first", cut, jnp.stack([target(half)]), hidden, w_down, (), cols)
        for step in range(1, half):
            got = ring.send(*sent)
            d = half - step
            blocks = jnp.stack([target(d), target(-d)])
            sent = down("second" if step == 1 else "middle", cut, blocks, hidden, w_down, got, cols)
        got = ring.send(*sent)
        results.append(
            down("last", cut, jnp.stack([target(0)]), hidden, w_down, got, cols, own=mixed)[0]
        )

    first = results[0].reshape(n, rows, cols)
    second = results[1][: n * rows].reshape(n, rows, cols)
    tail = results[1][n * rows : n * rows + n].reshape(n, 1, cols)
    return jnp.concatenate([first, second, tail], axis=1).reshape(n * (local + 1), cols)


def solution(mesh):
    in_specs = (
        P(("grp", "tok"), None),
        P(("grp", "tok"), None),
        P("grp", None),
        P(("grp", "tok"), None),
        P(("grp", "tok"), None, None),
        P(("grp", "tok")),
        P(),
        P("grp", "tok"),
        P(None, "tok"),
        P("grp", None),
        P(),
        P(None, "tok"),
        P(None, "tok"),
        P("tok", None),
    )
    out_specs = P("grp", "tok")
    return jax.shard_map(shards, mesh=mesh, in_specs=in_specs, out_specs=out_specs, check_vma=False)
```

```python
import functools
import math

import jax
import jax.numpy as jnp
from jax import lax
from jax.experimental import pallas as pl
from jax.experimental.pallas import tpu as pltpu
from jax.sharding import PartitionSpec as P

D = 4096
H = 32
KVH = 8
HD = 128
GROUP = H // KVH
WIDTH = KVH * HD
EPS = 1e-05
NEG = -1e30
Z_CHIPS = 4

HBM = pl.BlockSpec(memory_space=pltpu.HBM)
VMEM = pl.BlockSpec(memory_space=pltpu.VMEM)
SMEM = pl.BlockSpec(memory_space=pltpu.SMEM)
F32 = jnp.float32
BF16 = jnp.bfloat16


def ring_order(n):
    columns = n // Z_CHIPS
    if n % Z_CHIPS or columns % 2:
        return list(range(n))
    order = [z * columns for z in range(Z_CHIPS)]
    for i, z in enumerate(reversed(range(Z_CHIPS))):
        xs = range(1, columns) if i % 2 == 0 else range(columns - 1, 0, -1)
        order += [z * columns + x for x in xs]
    return order


def params(mib):
    return pltpu.CompilerParams(vmem_limit_bytes=mib * 2**20)


def cost(flops, moved, exps=0):
    return pl.CostEstimate(flops=int(flops), bytes_accessed=int(moved), transcendentals=int(exps))


def copies(pairs, sems):
    out = [pltpu.make_async_copy(src, dst, sems.at[i]) for i, (src, dst) in enumerate(pairs)]
    for c in out:
        c.start()
    return out


def row_parts(parts, owners, target, rows):
    n = len(parts) - 1
    half = n // 2
    pairs = []
    for i, part in enumerate(parts):
        d = i if i <= half else i - 1
        start = owners[d] * rows
        if i == half:
            pairs.append((part, target.at[pl.ds(pl.multiple_of(start, 16), rows // 2)]))
        elif i == half + 1:
            pairs.append((part, target.at[pl.ds(pl.multiple_of(start + rows // 2, 16), rows // 2)]))
        else:
            pairs.append((part, target.at[pl.ds(pl.multiple_of(start, 16), rows)]))
    return pairs


def attention_kernel(n, first, rows, owners, q_ref, seg_ref, *rest):
    parts, (out_ref, kv, sems) = rest[: n + 1], rest[-3:]
    total = kv.shape[0]
    moving = copies(row_parts(parts, owners, kv, total // n), sems)
    key_pos = lax.broadcasted_iota(jnp.int32, (rows, total), 1)
    query_pos = lax.broadcasted_iota(jnp.int32, (rows, total), 0) + (owners[0] * (total // n) + first)
    span = jnp.broadcast_to(seg_ref[...], (rows, total)).astype(F32)
    own_span = jnp.sum(jnp.where(key_pos == query_pos, span, 0.0), axis=-1, keepdims=True)
    seen = (key_pos <= query_pos) & (span == own_span)
    bias = jnp.where(seen, 0.0, NEG).astype(F32)
    bias = jnp.concatenate([bias] * GROUP, axis=0)
    for c in moving:
        c.wait()
    for k in range(KVH):
        q = jnp.concatenate(
            [q_ref[first : first + rows, (k * GROUP + g) * HD : (k * GROUP + g + 1) * HD] for g in range(GROUP)],
            axis=0,
        )
        s = lax.dot_general(
            q, kv[:, k * HD : (k + 1) * HD], (((1,), (1,)), ((), ())), preferred_element_type=F32
        )
        s = s * (1.0 / math.sqrt(HD)) + bias
        w = jnp.exp(s - jnp.max(s, axis=-1, keepdims=True)).astype(BF16)
        t = jnp.sum(w.astype(F32), axis=-1, keepdims=True)
        o = jnp.dot(w, kv[:, WIDTH + k * HD : WIDTH + (k + 1) * HD], preferred_element_type=F32) / t
        for g in range(GROUP):
            out_ref[:, (k * GROUP + g) * HD : (k * GROUP + g + 1) * HD] = o[g * rows : (g + 1) * rows].astype(BF16)


def attention(n, first, rows, owners, q, seg, parts):
    total = seg.shape[1]
    return pl.pallas_call(
        functools.partial(attention_kernel, n, first, rows),
        out_shape=jax.ShapeDtypeStruct((rows, D), BF16),
        in_specs=[SMEM, VMEM, VMEM] + [HBM] * (n + 1),
        out_specs=VMEM,
        scratch_shapes=[pltpu.VMEM((total, 2 * WIDTH), BF16), pltpu.SemaphoreType.DMA((n + 1,))],
        compiler_params=params(20),
        cost_estimate=cost(4 * rows * H * HD * total, 4 * total * WIDTH, rows * H * total),
        name="prefill_attention",
    )(owners, q, seg, *parts)


def decode_kernel(n, groups, meta, slots, length, q_ref, cache_ref, *rest):
    out_ref = rest[-1]
    positions = cache_ref.shape[1]
    tok, grp = meta[0], meta[n]
    request = slots[grp * n + tok]
    at = ((request % n) ^ tok) * groups + ((request // n) ^ grp)
    head = lax.broadcasted_iota(jnp.int32, (H, positions), 0) // GROUP
    q = q_ref[pl.ds(pl.multiple_of(at * H, H), H), :]
    s = jnp.zeros((H, positions), F32)
    for k in range(KVH):
        one = lax.dot_general(
            q, cache_ref[0, :, k * HD : (k + 1) * HD], (((1,), (1,)), ((), ())), preferred_element_type=F32
        )
        s = jnp.where(head == k, one, s)
    spot = lax.broadcasted_iota(jnp.int32, (H, positions), 1)
    s = jnp.where(spot < length[0], s * (1.0 / math.sqrt(HD)), NEG)
    w = jnp.exp(s - jnp.max(s, axis=-1, keepdims=True)).astype(BF16).astype(F32)
    t = jnp.sum(w, axis=-1, keepdims=True)
    o = jnp.zeros((H, HD), F32)
    for k in range(KVH):
        mine = jnp.where(head == k, w, 0.0).astype(BF16)
        o = o + jnp.dot(
            mine, cache_ref[0, :, WIDTH + k * HD : WIDTH + (k + 1) * HD], preferred_element_type=F32
        )
    out_ref[...] = (o / t).astype(BF16)


def decode(n, groups, meta, slots, length, q, cache):
    return pl.pallas_call(
        functools.partial(decode_kernel, n, groups),
        out_shape=jax.ShapeDtypeStruct((H, HD), BF16),
        in_specs=[SMEM, SMEM, SMEM, VMEM, VMEM],
        out_specs=VMEM,
        compiler_params=params(20),
        cost_estimate=cost(4 * H * WIDTH * cache.shape[1], 2 * cache.size, H * cache.shape[1]),
        name="decode_attention",
    )(meta, slots, length, q, cache)


def project_kernel(n, rows, extra, owners, *rest):
    if extra:
        dec_ref, perm_ref, rest = rest[0], rest[1], rest[2:]
    parts, (wo_ref, resid_ref) = rest[: n + 1], rest[n + 1 : n + 3]
    out_ref, x, w, sems, wsems = rest[-5:]
    moving = copies(row_parts(parts, owners, x, rows), sems)
    steps = 4
    deep = D // steps
    slabs = [pl.ds(i * deep, deep) for i in range(steps)]
    weights = copies([(wo_ref.at[s], w.at[s]) for s in slabs], wsems)
    if extra:
        x[n * rows :, :] = jnp.dot(perm_ref[...], dec_ref[...], preferred_element_type=F32).astype(BF16)
    for c in moving:
        c.wait()
    total = resid_ref[...].astype(F32)
    for i in range(steps):
        weights[i].wait()
        cut = slice(i * deep, (i + 1) * deep)
        total = total + jnp.dot(x[:, cut], w[cut, :], preferred_element_type=F32)
    out_ref[...] = total.astype(BF16)


def project(n, rows, owners, parts, wo, resid, dec=None, perm=None):
    m, cols = resid.shape
    extra = dec is not None
    return pl.pallas_call(
        functools.partial(project_kernel, n, rows, extra),
        out_shape=jax.ShapeDtypeStruct((m, cols), BF16),
        in_specs=[SMEM] + [VMEM] * (2 * extra) + [HBM] * (n + 2) + [VMEM],
        out_specs=VMEM,
        scratch_shapes=[
            pltpu.VMEM((m, D), BF16),
            pltpu.VMEM((D, cols), BF16),
            pltpu.SemaphoreType.DMA((n + 1,)),
            pltpu.SemaphoreType.DMA((4,)),
        ],
        compiler_params=params(20),
        cost_estimate=cost(2 * m * D * cols, 2 * D * (m + cols)),
        name="out_projection",
    )(owners, *([dec, perm] if extra else []), *parts, wo, resid)


def gate_up_kernel(n, cut, first, count, *rest):
    gate_ref, up_ref, rest = rest[0], rest[1], rest[2:]
    tile = 256
    w, wsems = rest[-2:]
    pairs = []
    for i in range(count):
        at = pl.ds((first + i) * tile, tile)
        pairs += [(gate_ref.at[:, at], w.at[2 * i]), (up_ref.at[:, at], w.at[2 * i + 1])]
    if first == 0:
        owners, tenants_ref, gain_ref = rest[:3]
        parts = rest[3 : 4 + n]
        normed_ref, out_ref, x, sems = rest[-6:-2]
        norm(n, cut, owners, tenants_ref, gain_ref, parts, normed_ref, x, sems, lambda: copies(pairs, wsems))
        weights = [pltpu.make_async_copy(src, dst, wsems.at[i]) for i, (src, dst) in enumerate(pairs)]
    else:
        normed_ref, out_ref = rest[0], rest[-3]
        weights = copies(pairs, wsems)
    for i in range(count):
        weights[2 * i].wait()
        gate = jnp.dot(normed_ref[...], w[2 * i], preferred_element_type=F32)
        weights[2 * i + 1].wait()
        lift = jnp.dot(normed_ref[...], w[2 * i + 1], preferred_element_type=F32)
        out_ref[:, i * tile : (i + 1) * tile] = (gate / (1.0 + jnp.exp(-gate)) * lift).astype(BF16)


def norm(n, cut, owners, tenants_ref, gain_ref, parts, out_ref, x, sems, meanwhile):
    m = x.shape[0]
    cols = D // n
    half = n // 2
    pairs = []
    for i, part in enumerate(parts):
        d = i if i <= half else i - 1
        at = pl.ds(pl.multiple_of(owners[d] * cols, 128), cols)
        if i == half:
            pairs.append((part, x.at[pl.ds(0, cut), at]))
        elif i == half + 1:
            pairs.append((part, x.at[pl.ds(cut, m - cut), at]))
        else:
            pairs.append((part, x.at[:, at]))
    moving = copies(pairs, sems)
    meanwhile()
    for c in moving:
        c.wait()
    square = jnp.zeros((m, 1), F32)
    for j in range(n):
        wide = x[:, j * cols : (j + 1) * cols].astype(F32)
        square = square + jnp.sum(wide * wide, axis=-1, keepdims=True)
    scale = lax.rsqrt(square / D + EPS)
    tenants = tenants_ref[...]
    for j in range(n):
        at = slice(j * cols, (j + 1) * cols)
        gain = jnp.broadcast_to(gain_ref[0:1, at], (m, cols))
        for t in range(1, gain_ref.shape[0]):
            gain = jnp.where(tenants == t, gain_ref[t : t + 1, at], gain)
        out_ref[:, at] = (x[:, at].astype(F32) * scale * gain).astype(BF16)


def norm_gate_up(n, cut, owners, tenants, gain, parts, w_gate, w_up, count):
    m = tenants.shape[0]
    tile = 256
    return pl.pallas_call(
        functools.partial(gate_up_kernel, n, cut, 0, count),
        out_shape=[jax.ShapeDtypeStruct((m, D), BF16), jax.ShapeDtypeStruct((m, count * tile), BF16)],
        in_specs=[HBM, HBM, SMEM, VMEM, VMEM] + [HBM] * (n + 1),
        out_specs=[VMEM, VMEM],
        scratch_shapes=[
            pltpu.VMEM((m, D), BF16),
            pltpu.SemaphoreType.DMA((n + 1,)),
            pltpu.VMEM((2 * count, D, tile), BF16),
            pltpu.SemaphoreType.DMA((2 * count,)),
        ],
        compiler_params=params(40),
        cost_estimate=cost(4 * m * D * count * tile, 4 * D * count * tile + 4 * m * D),
        name="norm_gate_up",
    )(w_gate, w_up, owners, tenants, gain, *parts)


def gate_up(normed, w_gate, w_up, first, count, owners):
    m = normed.shape[0]
    tile = 256
    return pl.pallas_call(
        functools.partial(gate_up_kernel, 0, 0, first, count),
        out_shape=jax.ShapeDtypeStruct((m, count * tile), BF16),
        in_specs=[HBM, HBM, VMEM, SMEM],
        out_specs=VMEM,
        scratch_shapes=[pltpu.VMEM((2 * count, D, tile), BF16), pltpu.SemaphoreType.DMA((2 * count,))],
        compiler_params=params(40),
        cost_estimate=cost(4 * m * D * count * tile, 4 * D * count * tile + 2 * m * D),
        name="gate_up",
    )(w_gate, w_up, normed, owners)


def len_outs(stage):
    return 1 if stage == "last" else 2


def down_kernel(stage, pieces, cut, blocks, given, owners, *rest):
    hidden, rest = rest[:pieces], rest[pieces:]
    two = stage in ("second", "middle")
    got = 0 if stage == "first" else 2
    w_ref, rest = rest[0], rest[1:]
    arrived, rest = rest[:got], rest[got:given] + rest[-(2 + len_outs(stage)) :]
    if stage == "last":
        own, rest = rest[0], rest[1:]
        outs, (w, sems) = rest[:1], rest[1:]
    else:
        outs, (w, sems) = rest[:2], rest[2:]
    cols = w.shape[-1]
    count = 2 if two else 1
    weights = copies(
        [
            (w_ref.at[:, pl.ds(pl.multiple_of(owners[blocks[i]] * cols, 128), cols)], w.at[i])
            for i in range(count)
        ],
        sems,
    )

    def block(i):
        weights[i].wait()
        total = None
        for j, h in enumerate(hidden):
            deep = h.shape[1]
            part = jnp.dot(h[...], w[i, j * deep : (j + 1) * deep, :], preferred_element_type=F32)
            total = part if total is None else total + part
        return total

    if stage == "first":
        total = block(0)
        outs[0][...] = total[:cut].astype(BF16)
        outs[1][...] = total[cut:].astype(BF16)
    elif stage == "second":
        total = block(0)
        outs[0][:cut] = (total[:cut] + arrived[0][...].astype(F32)).astype(BF16)
        outs[0][cut:] = total[cut:].astype(BF16)
        total = block(1)
        outs[1][:cut] = total[:cut].astype(BF16)
        outs[1][cut:] = (total[cut:] + arrived[1][...].astype(F32)).astype(BF16)
    elif stage == "middle":
        for i in range(2):
            outs[i][...] = (block(i) + arrived[i][...].astype(F32)).astype(BF16)
    else:
        total = block(0) + arrived[0][...].astype(F32) + arrived[1][...].astype(F32)
        outs[0][...] = (total + own[...].astype(F32)).astype(BF16)


def down(stage, cut, blocks, owners, hidden, w_down, arrived, cols, own=None):
    m = hidden[0].shape[0]
    deep = w_down.shape[0]
    two = stage in ("second", "middle")
    if stage == "first":
        shapes = [(cut, cols), (m - cut, cols)]
    elif two:
        shapes = [(m, cols)] * 2
    else:
        shapes = [(m, cols)]
    given = list(arrived) + ([own] if stage == "last" else [])
    return pl.pallas_call(
        functools.partial(down_kernel, stage, len(hidden), cut, blocks, len(given)),
        out_shape=[jax.ShapeDtypeStruct(s, BF16) for s in shapes],
        in_specs=[SMEM] + [VMEM] * len(hidden) + [HBM] + [VMEM] * len(given),
        out_specs=[VMEM] * len(shapes),
        scratch_shapes=[pltpu.VMEM((1 + two, deep, cols), BF16), pltpu.SemaphoreType.DMA((1 + two,))],
        compiler_params=params(20),
        cost_estimate=cost(2 * m * deep * cols * (1 + two), 2 * (1 + two) * deep * cols),
        name="down_" + stage,
    )(owners, *hidden, w_down, *given)


class Chain:
    def __init__(self, n, order, pair=None, cut=0):
        self.n, self.half, self.cut = n, n // 2, cut
        self.fw = [(order[i], order[(i + 1) % n]) for i in range(n)]
        self.bw = [(b, a) for a, b in self.fw]
        self.pair, self.ahead, self.behind = pair, [], []

    def done(self):
        return len(self.ahead) == self.half

    def parts(self, own):
        return [own] + self.ahead + self.behind[::-1]


class Order:
    def __init__(self, ids):
        self.ids, self.last = ids, ()

    def after(self):
        return lax.optimization_barrier((self.ids, *self.last))[0]

    def mark(self, *out):
        self.last = out
        return out[0] if len(out) == 1 else out

    def tied(self, *arrays):
        out = lax.optimization_barrier((*arrays, *self.last))[: len(arrays)]
        self.last = (out[0],)
        return out

    def send(self, chain, pair):
        pair = self.tied(*pair)
        return lax.ppermute(pair[0], "tok", chain.fw), lax.ppermute(pair[1], "tok", chain.bw)

    def hop(self, chain):
        if chain.done():
            return
        if len(chain.ahead) == chain.half - 1:
            chain.pair = (chain.pair[0][: chain.cut], chain.pair[1][chain.cut :])
        chain.pair = self.send(chain, chain.pair)
        chain.ahead.append(chain.pair[0])
        chain.behind.append(chain.pair[1])


class Exchange:
    def __init__(self, order, stack, bits):
        self.order, self.stack, self.bits = order, stack, list(bits)

    def step(self):
        if self.bits:
            axis, bit = self.bits.pop(0)
            pairs = [(i, i ^ bit) for i in range(lax.axis_size(axis))]
            (own,) = self.order.tied(self.stack)
            self.stack = jnp.concatenate([own, lax.ppermute(own, axis, pairs)], axis=0)


def shards(
    pre_q,
    pre_kv,
    pre_segment,
    dec_q,
    cache,
    cache_len,
    slot_request,
    resid,
    wo,
    tenant,
    norm_gain,
    w_gate,
    w_up,
    w_down,
):
    n, groups = lax.axis_size("tok"), lax.axis_size("grp")
    tok, grp = lax.axis_index("tok"), lax.axis_index("grp")
    local = pre_q.shape[0]
    rows = local // 2
    cols = wo.shape[1]
    half = n // 2
    lag = half // 2
    spare = -(-n // 16) * 16
    order = ring_order(n)
    ids = jnp.arange(n, dtype=jnp.int32)
    place = sum(jnp.where(tok == t, i, 0) for i, t in enumerate(order)).astype(jnp.int32)
    spots = (place - ids) % n
    owners = sum(jnp.where(spots == i, t, 0) for i, t in enumerate(order)).astype(jnp.int32)
    owners = jnp.concatenate([owners, jnp.reshape(grp, (1,)).astype(jnp.int32)])

    def split(a):
        a = a.reshape(n, local + 1, -1)
        first = a[:, :rows].reshape(n * rows, -1)
        second = a[:, rows:local].reshape(n * rows, -1)
        tail = jnp.pad(a[:, local], ((0, spare - n), (0, 0)))
        return first, jnp.concatenate([second, tail], axis=0)

    resids = split(resid)
    tenants = split(tenant[0][:, None])
    perm = (jnp.arange(spare)[:, None] == (tok ^ jnp.arange(spare))[None, :]).astype(BF16)

    def bits(axis, size):
        return [(axis, 1 << i) for i in range(size.bit_length() - 1)]

    run = Order(owners)
    queries = Exchange(run, dec_q.reshape(H, HD), bits("grp", groups) + bits("tok", n))
    keys = Chain(n, order, (pre_kv, pre_kv), local // 2)
    run.hop(keys)
    queries.step()
    queries.step()
    run.mark(*run.last, *resids, *tenants, owners, perm)
    run.hop(keys)
    while not keys.done():
        queries.step()
        run.hop(keys)
    queries.step()

    kv = keys.parts(pre_kv)
    own_a = run.mark(attention(n, 0, rows, run.after(), pre_q, pre_segment, kv))
    a = Chain(n, order, (own_a, own_a), rows // 2)
    run.hop(a)
    own_b = run.mark(attention(n, rows, rows, run.after(), pre_q, pre_segment, kv))
    while queries.bits:
        queries.step()
    own_dec = run.mark(
        decode(n, groups, run.after(), slot_request, cache_len, queries.stack, cache)
    )
    decs = Exchange(run, own_dec, bits("tok", n))
    b = Chain(n, order, (own_b, own_b), rows // 2)
    for _ in range(lag - 1):
        run.hop(a)
        decs.step()
    for _ in range(half - lag):
        run.hop(a)
        decs.step()
        run.hop(b)
    mixed_a = run.mark(project(n, rows, run.after(), a.parts(own_a), wo, resids[0]))
    cut_a = (mixed_a.shape[0] // 32) * 16
    g = Chain(n, order, (mixed_a, mixed_a), cut_a)
    for _ in range(lag):
        run.hop(g)
        decs.step()
        run.hop(b)
    run.hop(g)
    while decs.bits:
        decs.step()
    dec_all = jnp.pad(decs.stack.reshape(n, D), ((0, spare - n), (0, 0)))
    mixed_b = run.mark(project(n, rows, run.after(), b.parts(own_b), wo, resids[1], dec_all, perm))
    cut_b = (mixed_b.shape[0] // 32) * 16
    h = Chain(n, order, (mixed_b, mixed_b), cut_b)
    for _ in range(half - lag):
        run.hop(h)
        run.hop(g)

    tiles = w_gate.shape[1] // 256
    one = (tiles + 1) // 2

    def feed(c, chain, own):
        out = norm_gate_up(
            n, chain.cut, run.after(), tenants[c], norm_gain, chain.parts(own), w_gate, w_up, one
        )
        run.mark(out[1])
        return out

    def rest(normed):
        return run.mark(gate_up(normed, w_gate, w_up, one, tiles - one, run.after()))

    def block(d):
        return (-d) % n

    class Sum:
        def __init__(self, hidden, own, cut):
            self.hidden, self.own, self.cut = hidden, own, cut
            self.chain, self.step = Chain(n, order), 0

        def done(self):
            return self.step == half

        def call(self, stage, blocks, arrived, own=None):
            out = down(stage, self.cut, blocks, run.after(), self.hidden, w_down, arrived, cols, own=own)
            run.mark(out[0])
            return out

        def hop(self):
            if self.done():
                return
            d = half - self.step
            if self.step == 0:
                out = self.call("first", [block(half)], ())
            else:
                stage = "second" if self.step == 1 else "middle"
                out = self.call(stage, [block(d), block(-d)], self.arrived)
            self.arrived = run.send(self.chain, out)
            self.step += 1

        def finish(self):
            return self.call("last", [0], self.arrived, self.own)[0]

    normed_a, hid_a1 = feed(0, g, mixed_a)
    for _ in range(lag // 2):
        run.hop(h)
    hid_a2 = rest(normed_a)
    while not h.done():
        run.hop(h)
    sum_a = Sum([hid_a1, hid_a2], mixed_a, cut_a)
    sum_a.hop()
    normed_b, hid_b1 = feed(1, h, mixed_b)
    sum_a.hop()
    hid_b2 = rest(normed_b)
    sum_b = Sum([hid_b1, hid_b2], mixed_b, cut_b)
    while not sum_a.done():
        sum_a.hop()
        sum_b.hop()
    out_a = sum_a.finish()
    while not sum_b.done():
        sum_b.hop()
    out_b = sum_b.finish()

    top = out_a.reshape(n, rows, cols)
    low = out_b[: n * rows].reshape(n, rows, cols)
    tail = out_b[n * rows : n * rows + n].reshape(n, 1, cols)
    return jnp.concatenate([top, low, tail], axis=1).reshape(n * (local + 1), cols)


def solution(mesh):
    in_specs = (
        P(("grp", "tok"), None),
        P(("grp", "tok"), None),
        P("grp", None),
        P(("grp", "tok"), None),
        P(("grp", "tok"), None, None),
        P(("grp", "tok")),
        P(),
        P("grp", "tok"),
        P(None, "tok"),
        P("grp", None),
        P(),
        P(None, "tok"),
        P(None, "tok"),
        P("tok", None),
    )
    out_specs = P("grp", "tok")
    return jax.shard_map(shards, mesh=mesh, in_specs=in_specs, out_specs=out_specs, check_vma=False)
```

```python
import functools
import math

import jax
import jax.numpy as jnp
from jax import lax
from jax.experimental import pallas as pl
from jax.experimental.pallas import tpu as pltpu
from jax.sharding import PartitionSpec as P

D = 4096
H = 32
KVH = 8
HD = 128
GROUP = H // KVH
WIDTH = KVH * HD
EPS = 1e-05
NEG = -1e30
Z_CHIPS = 4

HBM = pl.BlockSpec(memory_space=pltpu.HBM)
VMEM = pl.BlockSpec(memory_space=pltpu.VMEM)
SMEM = pl.BlockSpec(memory_space=pltpu.SMEM)
F32 = jnp.float32
BF16 = jnp.bfloat16


def ring_order(n):
    columns = n // Z_CHIPS
    if n % Z_CHIPS or columns % 2:
        return list(range(n))
    order = [z * columns for z in range(Z_CHIPS)]
    for i, z in enumerate(reversed(range(Z_CHIPS))):
        xs = range(1, columns) if i % 2 == 0 else range(columns - 1, 0, -1)
        order += [z * columns + x for x in xs]
    return order


def params(mib):
    return pltpu.CompilerParams(vmem_limit_bytes=mib * 2**20)


STEP = pl.CostEstimate(flops=500_000_000, bytes_accessed=1_000_000, transcendentals=0)


def copies(pairs, sems):
    out = [pltpu.make_async_copy(src, dst, sems.at[i]) for i, (src, dst) in enumerate(pairs)]
    for c in out:
        c.start()
    return out


def spread(parts, owners, target, rows):
    n, half = len(parts), len(parts) // 2
    pairs = []
    for i, part in enumerate(parts):
        d = i if n % 2 == 0 or i <= half else i - 1
        start, size = owners[d] * rows, rows
        if n % 2 and d == half:
            start, size = start + (i - half) * (rows // 2), rows // 2
        pairs.append((part, target.at[pl.ds(pl.multiple_of(start, 16), size)]))
    return pairs


def attention_kernel(count, first, rows, owners, q_in, seg_ref, *rest):
    parts, (out_ref, kv, q, sems) = rest[:count], rest[-4:]
    total = kv.shape[0]
    local = q_in.shape[0]
    moving = copies(spread(parts, owners, kv, local) + [(q_in.at[pl.ds(first, rows)], q)], sems)
    key_pos = lax.broadcasted_iota(jnp.int32, (rows, total), 1)
    query_pos = lax.broadcasted_iota(jnp.int32, (rows, total), 0) + (owners[0] * local + first)
    span = jnp.broadcast_to(seg_ref[...], (rows, total)).astype(F32)
    own_span = jnp.sum(jnp.where(key_pos == query_pos, span, 0.0), axis=-1, keepdims=True)
    seen = (key_pos <= query_pos) & (span == own_span)
    bias = jnp.where(seen, 0.0, NEG).astype(F32)
    bias = jnp.concatenate([bias] * GROUP, axis=0)
    if len(rest) > count + 4:
        out_ref[H * rows :, :] = rest[count][...]
    for c in moving:
        c.wait()
    for k in range(KVH):
        heads = range(k * GROUP, (k + 1) * GROUP)
        four = jnp.concatenate([q[:, i * HD : (i + 1) * HD] for i in heads], axis=0)
        s = lax.dot_general(
            four, kv[:, k * HD : (k + 1) * HD], (((1,), (1,)), ((), ())), preferred_element_type=F32
        )
        s = s * (1.0 / math.sqrt(HD)) + bias
        w = jnp.exp(s - jnp.max(s, axis=-1, keepdims=True)).astype(BF16)
        t = jnp.sum(w.astype(F32), axis=-1, keepdims=True)
        o = jnp.dot(w, kv[:, WIDTH + k * HD : WIDTH + (k + 1) * HD], preferred_element_type=F32) / t
        out_ref[k * GROUP * rows : (k + 1) * GROUP * rows, :] = o.astype(BF16)


def attention(first, rows, owners, q, seg, parts, dec=()):
    total = seg.shape[1]
    return pl.pallas_call(
        functools.partial(attention_kernel, len(parts), first, rows),
        out_shape=jax.ShapeDtypeStruct((H * (rows + len(dec)), HD), BF16),
        in_specs=[SMEM, HBM, VMEM] + [VMEM] * (len(parts) + len(dec)),
        out_specs=VMEM,
        scratch_shapes=[
            pltpu.VMEM((total, 2 * WIDTH), BF16),
            pltpu.VMEM((rows, D), BF16),
            pltpu.SemaphoreType.DMA((len(parts) + 1,)),
        ],
        compiler_params=params(40),
        cost_estimate=STEP,
        name="prefill_attention",
    )(owners, q, seg, *parts, *dec)


def decode_kernel(n, groups, owners, slots, length, cache_in, *rest):
    parts, (out_ref, stack, cache_ref, sems) = rest[:n], rest[n:]
    positions = cache_ref.shape[1]
    moving = copies(spread(parts, owners, stack, groups * H) + [(cache_in, cache_ref)], sems)
    tok, grp = owners[0], owners[n]
    request = slots[grp * n + tok]
    at = (request % n) * groups + ((request // n) ^ grp)
    head = lax.broadcasted_iota(jnp.int32, (H, positions), 0) // GROUP
    for c in moving:
        c.wait()
    q = stack[pl.ds(pl.multiple_of(at * H, H), H), :]
    s = jnp.zeros((H, positions), F32)
    for k in range(KVH):
        one = lax.dot_general(
            q, cache_ref[0, :, k * HD : (k + 1) * HD], (((1,), (1,)), ((), ())), preferred_element_type=F32
        )
        s = jnp.where(head == k, one, s)
    spot = lax.broadcasted_iota(jnp.int32, (H, positions), 1)
    s = jnp.where(spot < length[0], s * (1.0 / math.sqrt(HD)), NEG)
    w = jnp.exp(s - jnp.max(s, axis=-1, keepdims=True)).astype(BF16).astype(F32)
    t = jnp.sum(w, axis=-1, keepdims=True)
    o = jnp.zeros((H, HD), F32)
    for k in range(KVH):
        mine = jnp.where(head == k, w, 0.0).astype(BF16)
        o = o + jnp.dot(
            mine, cache_ref[0, :, WIDTH + k * HD : WIDTH + (k + 1) * HD], preferred_element_type=F32
        )
    out_ref[...] = (o / t).astype(BF16)


def decode(n, groups, owners, slots, length, parts, cache):
    return pl.pallas_call(
        functools.partial(decode_kernel, n, groups),
        out_shape=jax.ShapeDtypeStruct((H, HD), BF16),
        in_specs=[SMEM, SMEM, SMEM, HBM] + [VMEM] * n,
        out_specs=VMEM,
        scratch_shapes=[
            pltpu.VMEM((n * groups * H, HD), BF16),
            pltpu.VMEM(cache.shape, BF16),
            pltpu.SemaphoreType.DMA((n + 1,)),
        ],
        compiler_params=params(40),
        cost_estimate=STEP,
        name="decode_attention",
    )(owners, slots, length, cache, *parts)


def project_kernel(n, rows, owners, *rest):
    parts, (wo_ref, resid_ref, out_ref, x, dec) = rest[:n], rest[n:]
    for d, part in enumerate(parts):
        at = pl.ds(pl.multiple_of(owners[d] * rows, 16), rows)
        for i in range(H):
            x[at, i * HD : (i + 1) * HD] = part[i * rows : (i + 1) * rows, :]
        if part.shape[0] > H * rows:
            dec[pl.ds(pl.multiple_of(owners[d] * H, H), H), :] = part[H * rows :, :]
    spare = x.shape[0] - n * rows
    if spare:
        at = lax.broadcasted_iota(jnp.int32, (H * spare, n * H), 0)
        of = lax.broadcasted_iota(jnp.int32, (H * spare, n * H), 1)
        pick = jnp.where(of == (at % spare) * H + at // spare, 1.0, 0.0).astype(BF16)
        heads = jnp.dot(pick, dec[...], preferred_element_type=F32).astype(BF16)
        for i in range(H):
            x[n * rows :, i * HD : (i + 1) * HD] = heads[i * spare : (i + 1) * spare]
    total = jnp.dot(x[...], wo_ref[...], preferred_element_type=F32)
    out_ref[...] = (resid_ref[...].astype(F32) + total).astype(BF16)


def project(rows, owners, parts, wo, resid):
    m, cols = resid.shape
    n = len(parts)
    return pl.pallas_call(
        functools.partial(project_kernel, n, rows),
        out_shape=jax.ShapeDtypeStruct((m, cols), BF16),
        in_specs=[SMEM] + [VMEM] * (n + 2),
        out_specs=VMEM,
        scratch_shapes=[pltpu.VMEM((m, D), BF16), pltpu.VMEM((n * H, HD), BF16)],
        compiler_params=params(16),
        cost_estimate=STEP,
        name="out_projection",
    )(owners, *parts, wo, resid)


def gate_kernel(taken, shares, owners, tenants_ref, gain_ref, w_ref, *rest):
    parts, rest = rest[: 2 * len(shares)], rest[2 * len(shares) :]
    if taken:
        held, squares, rest = rest[0], rest[1], rest[2:]
    out, squares_out, scaled, w, sems = rest
    cols = w.shape[1]
    m = out.shape[0]
    places = [pl.ds(pl.multiple_of(owners[s] * cols, cols), cols) for s in shares]
    weights = copies([(w_ref.at[at], w.at[i]) for i, at in enumerate(places)], sems)
    tenants = tenants_ref[...]
    total = squares[...] if taken else jnp.zeros((m, HD), F32)
    for i, at in enumerate(places):
        x = jnp.concatenate([p[...] for p in parts[2 * i : 2 * i + 2]], axis=0).astype(F32)
        for j in range(0, cols, HD):
            total = total + x[:, j : j + HD] * x[:, j : j + HD]
        gain = jnp.broadcast_to(gain_ref[0:1, at], (m, cols))
        for t in range(1, gain_ref.shape[0]):
            gain = jnp.where(tenants == t, gain_ref[t : t + 1, at], gain)
        scaled[:, i * cols : (i + 1) * cols] = (x * gain).astype(BF16)
    squares_out[...] = total
    accumulate(out, held if taken else None, scaled, w, weights)


def up_kernel(taken, shares, owners, w_ref, scaled, *rest):
    if taken:
        held, rest = rest[0], rest[1:]
    out, w, sems = rest
    cols = w.shape[1]
    places = [pl.ds(pl.multiple_of(owners[s] * cols, cols), cols) for s in shares]
    weights = copies([(w_ref.at[at], w.at[i]) for i, at in enumerate(places)], sems)
    accumulate(out, held if taken else None, scaled, w, weights)


def accumulate(out, held, scaled, w, weights):
    cols = w.shape[1]
    for i, copy in enumerate(weights):
        copy.wait()
        one = jnp.dot(scaled[:, i * cols : (i + 1) * cols], w[i], preferred_element_type=F32)
        if i == 0:
            out[...] = one if held is None else held[...] + one
        else:
            out[...] += one


def gate_step(shares, owners, tenants, gain, w_gate, parts, held):
    m, wide = tenants.shape[0], w_gate.shape[1]
    cols = parts[0].shape[1]
    first = 4 + len(parts)
    return pl.pallas_call(
        functools.partial(gate_kernel, len(held) > 0, shares),
        out_shape=[
            jax.ShapeDtypeStruct((m, wide), F32),
            jax.ShapeDtypeStruct((m, HD), F32),
            jax.ShapeDtypeStruct((m, cols * len(shares)), BF16),
        ],
        in_specs=[SMEM, VMEM, VMEM, HBM] + [VMEM] * (len(parts) + len(held)),
        out_specs=[VMEM] * 3,
        scratch_shapes=[
            pltpu.VMEM((len(shares), cols, wide), BF16),
            pltpu.SemaphoreType.DMA((len(shares),)),
        ],
        input_output_aliases={first: 0, first + 1: 1} if held else {},
        compiler_params=params(46),
        cost_estimate=STEP,
        name="gate_sum",
    )(owners, tenants, gain, w_gate, *parts, *held)


def up_step(shares, owners, w_up, scaled, held):
    m, wide = scaled.shape[0], w_up.shape[1]
    cols = scaled.shape[1] // len(shares)
    return pl.pallas_call(
        functools.partial(up_kernel, len(held) > 0, shares),
        out_shape=jax.ShapeDtypeStruct((m, wide), F32),
        in_specs=[SMEM, HBM, VMEM] + [VMEM] * len(held),
        out_specs=VMEM,
        scratch_shapes=[
            pltpu.VMEM((len(shares), cols, wide), BF16),
            pltpu.SemaphoreType.DMA((len(shares),)),
        ],
        input_output_aliases={3: 0} if held else {},
        compiler_params=params(46),
        cost_estimate=STEP,
        name="up_sum",
    )(owners, w_up, scaled, *held)


def hidden_kernel(lo, hi, share, owners, tenants_ref, gain_ref, gate_ref, up_ref, part, gates, lifts, squares, out, w, sems):
    cols = w.shape[1]
    m = hi - lo
    at = pl.ds(pl.multiple_of(owners[share] * cols, cols), cols)
    weights = copies([(gate_ref.at[at], w.at[0]), (up_ref.at[at], w.at[1])], sems)
    tenants = tenants_ref[lo:hi, :]
    x = part[...].astype(F32)
    total = squares[lo:hi, :]
    for j in range(0, cols, HD):
        total = total + x[:, j : j + HD] * x[:, j : j + HD]
    gain = jnp.broadcast_to(gain_ref[0:1, at], (m, cols))
    for t in range(1, gain_ref.shape[0]):
        gain = jnp.where(tenants == t, gain_ref[t : t + 1, at], gain)
    scaled = (x * gain).astype(BF16)
    scale = lax.rsqrt(jnp.sum(total, axis=-1, keepdims=True) / D + EPS)
    weights[0].wait()
    gate = (gates[lo:hi, :] + jnp.dot(scaled, w[0], preferred_element_type=F32)) * scale
    gate = gate / (1.0 + jnp.exp(-gate))
    weights[1].wait()
    lift = (lifts[lo:hi, :] + jnp.dot(scaled, w[1], preferred_element_type=F32)) * scale
    out[...] = (gate * lift).astype(BF16)


def hidden_step(lo, hi, share, owners, tenants, gain, w_gate, w_up, part, held):
    wide = w_gate.shape[1]
    return pl.pallas_call(
        functools.partial(hidden_kernel, lo, hi, share),
        out_shape=jax.ShapeDtypeStruct((hi - lo, wide), BF16),
        in_specs=[SMEM, VMEM, VMEM, HBM, HBM] + [VMEM] * 4,
        out_specs=VMEM,
        scratch_shapes=[
            pltpu.VMEM((2, part.shape[1], wide), BF16),
            pltpu.SemaphoreType.DMA((2,)),
        ],
        compiler_params=params(46),
        cost_estimate=STEP,
        name="hidden",
    )(owners, tenants, gain, w_gate, w_up, part, *held)


def pause_kernel(ids, out):
    for i in range(ids.shape[0]):
        out[i] = ids[i]


def pause(ids):
    return pl.pallas_call(
        pause_kernel,
        out_shape=jax.ShapeDtypeStruct(ids.shape, ids.dtype),
        in_specs=[SMEM],
        out_specs=SMEM,
        cost_estimate=STEP,
        name="step",
    )(ids)


def down_kernel(blocks, flags, own, owners, hidden, w_ref, *rest):
    terms, rest = rest[: sum(flags) + own], rest[sum(flags) + own :]
    outs, (w, sems) = rest[: len(blocks)], rest[len(blocks) :]
    cols = w.shape[-1]
    weights = copies(
        [
            (w_ref.at[:, pl.ds(pl.multiple_of(owners[b] * cols, HD), cols)], w.at[i])
            for i, b in enumerate(blocks)
        ],
        sems,
    )
    taken = 0
    for i in range(len(blocks)):
        weights[i].wait()
        total = jnp.dot(hidden[...], w[i], preferred_element_type=F32)
        for term in terms[taken : taken + flags[i] + own]:
            total = total + term[...].astype(F32)
        taken += flags[i]
        outs[i][...] = total.astype(BF16)


def down(blocks, flags, owners, hidden, w_down, arrived, cols, own=()):
    m, deep = hidden.shape
    count = len(blocks)
    return pl.pallas_call(
        functools.partial(down_kernel, blocks, flags, len(own)),
        out_shape=[jax.ShapeDtypeStruct((m, cols), BF16) for _ in blocks],
        in_specs=[SMEM, VMEM, HBM] + [VMEM] * (len(arrived) + len(own)),
        out_specs=[VMEM] * count,
        scratch_shapes=[pltpu.VMEM((count, deep, cols), BF16), pltpu.SemaphoreType.DMA((count,))],
        compiler_params=params(50),
        cost_estimate=STEP,
        name="down_sum",
    )(owners, hidden, w_down, *arrived, *own)


class Chain:
    def __init__(self, n, order, own, last):
        self.n, self.half, self.last = n, n // 2, last
        self.fw = [(order[i], order[(i + 1) % n]) for i in range(n)]
        self.bw = [(b, a) for a, b in self.fw]
        self.own, self.ahead, self.behind, self.hops = own, [own], [own], 0

    def done(self):
        return self.hops == self.half

    def parts(self):
        return [self.own] + self.ahead[1:] + self.behind[:0:-1]


class Order:
    def __init__(self, ids):
        self.ids, self.last = ids, ()

    def after(self):
        return lax.optimization_barrier((self.ids, *self.last))[0]

    def mark(self, *out):
        self.last = out
        return out[0]

    def tied(self, *arrays):
        out = lax.optimization_barrier((*arrays, *self.last))[: len(arrays)]
        self.last = (out[0],)
        return out

    def hop(self, chain):
        chain.hops += 1
        f, b = chain.ahead[-1], chain.behind[-1]
        if chain.done() and chain.last == "split":
            cut = f.shape[0] // 2
            f, b = f[:cut], b[cut:]
        if chain.done() and chain.last == "fw":
            (f,) = self.tied(f)
            chain.ahead.append(lax.ppermute(f, "tok", chain.fw))
        elif chain.done() and chain.last == "bw":
            (b,) = self.tied(b)
            chain.behind.append(lax.ppermute(b, "tok", chain.bw))
        else:
            f, b = self.tied(f, b)
            chain.ahead.append(lax.ppermute(f, "tok", chain.fw))
            chain.behind.append(lax.ppermute(b, "tok", chain.bw))


class Sum:
    def __init__(self, run, chain, hidden, w_down, cols, own):
        self.run, self.chain, self.hidden, self.w_down = run, chain, hidden, w_down
        self.cols, self.own, self.step, self.arrived = cols, own, 0, ()

    def call(self, blocks, flags, own=()):
        blocks = [-b % self.chain.n for b in blocks]
        out = down(blocks, flags, self.run.after(), self.hidden, self.w_down, self.arrived, self.cols, own)
        self.run.mark(out[0])
        return out

    def hop(self):
        chain = self.chain
        d, forward = chain.half - self.step, chain.last == "fw"
        if self.step == 0:
            out = self.run.tied(*self.call([d], [0]))
            self.arrived = (lax.ppermute(out[0], "tok", chain.fw if forward else chain.bw),)
        else:
            flags = [1, 1] if self.step > 1 else ([1, 0] if forward else [0, 1])
            out = self.run.tied(*self.call([d, -d], flags))
            self.arrived = (lax.ppermute(out[0], "tok", chain.fw), lax.ppermute(out[1], "tok", chain.bw))
        self.step += 1

    def finish(self):
        return self.call([0], [2], (self.own,))[0]


def shards(
    pre_q,
    pre_kv,
    pre_segment,
    dec_q,
    cache,
    cache_len,
    slot_request,
    resid,
    wo,
    tenant,
    norm_gain,
    w_gate,
    w_up,
    w_down,
):
    n, groups = lax.axis_size("tok"), lax.axis_size("grp")
    tok, grp = lax.axis_index("tok"), lax.axis_index("grp")
    local = pre_q.shape[0]
    rows = local // 2
    cols = wo.shape[1]
    half = n // 2
    spare = -(-n // 16) * 16
    order = ring_order(n)
    ids = jnp.arange(n, dtype=jnp.int32)
    place = sum(jnp.where(tok == t, i, 0) for i, t in enumerate(order)).astype(jnp.int32)
    spots = (place - ids) % n
    owners = sum(jnp.where(spots == i, t, 0) for i, t in enumerate(order)).astype(jnp.int32)
    owners = jnp.concatenate([owners, jnp.reshape(grp, (1,)).astype(jnp.int32)])

    def split(a):
        a = a.reshape(n, local + 1, -1)
        first = a[:, :rows].reshape(n * rows, -1)
        second = a[:, rows:local].reshape(n * rows, -1)
        tail = jnp.pad(a[:, local], ((0, spare - n), (0, 0)))
        return first, jnp.concatenate([second, tail], axis=0)

    resids = split(resid)
    tenants = jnp.concatenate(split(tenant[0][:, None]), axis=0)
    run = Order(owners)

    def chain(own, last):
        return Chain(n, order, own, last)

    keys = chain(pre_kv, "split")
    run.hop(keys)
    queries = dec_q.reshape(H, HD)
    for i in range(groups.bit_length() - 1):
        pairs = [(j, j ^ (1 << i)) for j in range(groups)]
        (queries,) = run.tied(queries)
        queries = jnp.concatenate([queries, lax.ppermute(queries, "grp", pairs)], axis=0)
    run.mark(*run.last, *resids, tenants, owners)
    asks = chain(queries, "fw")
    while not keys.done():
        run.hop(keys)
        run.hop(asks)
    run.hop(asks)

    kv = keys.parts()
    a = chain(run.mark(attention(0, rows, run.after(), pre_q, pre_segment, kv)), "fw")
    run.hop(a)
    dec = run.mark(decode(n, groups, run.after(), slot_request, cache_len, asks.parts(), cache))
    b = chain(run.mark(attention(rows, rows, run.after(), pre_q, pre_segment, kv, (dec,))), "bw")
    run.hop(b)
    while not a.done():
        run.mark(pause(run.after()))
        run.hop(a)
        run.mark(pause(run.after()))
        run.hop(b)

    mixed_a = run.mark(project(rows, run.after(), a.parts(), wo, resids[0]))
    g = chain(mixed_a, "fw")
    run.hop(g)
    mixed_b = run.mark(project(rows, run.after(), b.parts(), wo, resids[1]))
    h = chain(mixed_b, "bw")
    run.hop(h)

    m_a, m = mixed_a.shape[0], tenants.shape[0]
    gates, lifts = (), ()
    for i in range(half):
        if i:
            shares, parts = [i, n - i], [g.ahead[i], h.ahead[i], g.behind[i], h.behind[i]]
        else:
            shares, parts = [0], [mixed_a, mixed_b]
        out = gate_step(shares, run.after(), tenants, norm_gain, w_gate, parts, gates)
        gates, scaled = out[:2], out[2]
        run.mark(scaled)
        if i + 1 < half:
            run.hop(g)
        lifts = (run.mark(up_step(shares, run.after(), w_up, scaled, lifts)),)
        if i + 1 < half:
            run.hop(h)

    def hide(lo, hi, part):
        held = (gates[0], lifts[0], gates[1])
        return run.mark(
            hidden_step(lo, hi, half, run.after(), tenants, norm_gain, w_gate, w_up, part, held)
        )

    hid_a = hide(0, m_a, g.ahead[half])
    sum_a = Sum(run, g, hid_a, w_down, cols, mixed_a)
    sum_a.hop()
    hid_b = hide(m_a, m, h.behind[half])
    sum_b = Sum(run, h, hid_b, w_down, cols, mixed_b)
    sum_b.hop()
    for _ in range(1, half):
        sum_a.hop()
        sum_b.hop()
    out_a = sum_a.finish()
    out_b = sum_b.finish()

    top = out_a.reshape(n, rows, cols)
    low = out_b[: n * rows].reshape(n, rows, cols)
    tail = out_b[n * rows : n * rows + n].reshape(n, 1, cols)
    return jnp.concatenate([top, low, tail], axis=1).reshape(n * (local + 1), cols)


def solution(mesh):
    in_specs = (
        P(("grp", "tok"), None),
        P(("grp", "tok"), None),
        P("grp", None),
        P(("grp", "tok"), None),
        P(("grp", "tok"), None, None),
        P(("grp", "tok")),
        P(),
        P("grp", "tok"),
        P(None, "tok"),
        P("grp", None),
        P(),
        P(None, "tok"),
        P(None, "tok"),
        P("tok", None),
    )
    out_specs = P("grp", "tok")
    return jax.shard_map(shards, mesh=mesh, in_specs=in_specs, out_specs=out_specs, check_vma=False)
```

```python
import functools
import math

import jax
import jax.numpy as jnp
from jax import lax
from jax.experimental import pallas as pl
from jax.experimental.pallas import tpu as pltpu
from jax.sharding import PartitionSpec as P

D = 4096
H = 32
KVH = 8
HD = 128
GROUP = H // KVH
WIDTH = KVH * HD
EPS = 1e-05
NEG = -1e30
Z_CHIPS = 4

HBM = pl.BlockSpec(memory_space=pltpu.HBM)
VMEM = pl.BlockSpec(memory_space=pltpu.VMEM)
SMEM = pl.BlockSpec(memory_space=pltpu.SMEM)
F32 = jnp.float32
BF16 = jnp.bfloat16


def ring_order(n):
    columns = n // Z_CHIPS
    if n % Z_CHIPS or columns % 2:
        return list(range(n))
    order = [z * columns for z in range(Z_CHIPS)]
    for i, z in enumerate(reversed(range(Z_CHIPS))):
        xs = range(1, columns) if i % 2 == 0 else range(columns - 1, 0, -1)
        order += [z * columns + x for x in xs]
    return order


def params(mib):
    return pltpu.CompilerParams(vmem_limit_bytes=mib * 2**20)


STEP = pl.CostEstimate(flops=500_000_000, bytes_accessed=1_000_000, transcendentals=0)


def copies(pairs, sems):
    out = [pltpu.make_async_copy(src, dst, sems.at[i]) for i, (src, dst) in enumerate(pairs)]
    for c in out:
        c.start()
    return out


def pack_kernel(kv_ref, ask_ref, out_ref):
    rows, width = kv_ref.shape
    for i in range(width // HD):
        out_ref[i * rows : (i + 1) * rows, :] = kv_ref[:, i * HD : (i + 1) * HD]
    ask = ask_ref[...].astype(F32)
    heads = jnp.concatenate([ask[:, i * HD : (i + 1) * HD] for i in range(H)], axis=0)
    out_ref[rows * (width // HD) :, :] = heads.astype(BF16)


def pack(kv, ask):
    rows, count = kv.shape[0], kv.shape[1] // HD
    return pl.pallas_call(
        pack_kernel,
        out_shape=jax.ShapeDtypeStruct((count * rows + H, HD), BF16),
        in_specs=[VMEM, VMEM],
        out_specs=VMEM,
        cost_estimate=STEP,
        name="pack_keys",
    )(kv, ask)


def pieces(parts, rows):
    half = len(parts) // 2
    out = []
    for i, part in enumerate(parts):
        if i == half:
            out.append((half, part, 0, range(KVH)))
        elif i == half + 1:
            out.append((half, part, -KVH * rows, range(KVH, 2 * KVH)))
        else:
            out.append((i if i < half else i - 1, part, 0, range(2 * KVH)))
    return out


def attention_kernel(count, first, rows, owners, q_in, seg_ref, *rest):
    parts, (out_ref, kv, q, sems) = rest[:count], rest[-4:]
    total = kv.shape[1]
    local = q_in.shape[0]
    moving = copies([(q_in.at[pl.ds(first, rows)], q)], sems)
    for d, part, offset, heads in pieces(parts, local):
        at = pl.ds(pl.multiple_of(owners[d] * local, 16), local)
        for i in heads:
            kv[i, at, :] = part[offset + i * local : offset + (i + 1) * local, :]
    key_pos = lax.broadcasted_iota(jnp.int32, (rows, total), 1)
    query_pos = lax.broadcasted_iota(jnp.int32, (rows, total), 0) + (owners[0] * local + first)
    span = jnp.broadcast_to(seg_ref[...], (rows, total)).astype(F32)
    own_span = jnp.sum(jnp.where(key_pos == query_pos, span, 0.0), axis=-1, keepdims=True)
    seen = (key_pos <= query_pos) & (span == own_span)
    bias = jnp.where(seen, 0.0, NEG).astype(F32)
    bias = jnp.concatenate([bias] * GROUP, axis=0)
    if len(rest) > count + 4:
        out_ref[H * rows :, :] = rest[count][...]
    moving[0].wait()
    for k in range(KVH):
        heads = range(k * GROUP, (k + 1) * GROUP)
        four = jnp.concatenate([q[:, i * HD : (i + 1) * HD] for i in heads], axis=0)
        s = lax.dot_general(four, kv[k], (((1,), (1,)), ((), ())), preferred_element_type=F32)
        s = s * (1.0 / math.sqrt(HD)) + bias
        w = jnp.exp(s - jnp.max(s, axis=-1, keepdims=True)).astype(BF16)
        t = jnp.sum(w.astype(F32), axis=-1, keepdims=True)
        o = jnp.dot(w, kv[KVH + k], preferred_element_type=F32) / t
        out_ref[k * GROUP * rows : (k + 1) * GROUP * rows, :] = o.astype(BF16)


def attention(first, rows, owners, q, seg, parts, dec=()):
    total = seg.shape[1]
    return pl.pallas_call(
        functools.partial(attention_kernel, len(parts), first, rows),
        out_shape=jax.ShapeDtypeStruct((H * (rows + len(dec)), HD), BF16),
        in_specs=[SMEM, HBM, VMEM] + [VMEM] * (len(parts) + len(dec)),
        out_specs=VMEM,
        scratch_shapes=[
            pltpu.VMEM((2 * KVH, total, HD), BF16),
            pltpu.VMEM((rows, D), BF16),
            pltpu.SemaphoreType.DMA((1,)),
        ],
        compiler_params=params(40),
        cost_estimate=STEP,
        name="prefill_attention",
    )(owners, q, seg, *parts, *dec)


def pick_kernel(n, groups, owners, slots, *rest):
    parts, outs = rest[: n + 1], rest[n + 1 :]
    tok, grp = owners[0], owners[n]
    for j in range(groups):
        request = slots[(grp ^ j) * n + tok]
        for i, part in enumerate(parts):
            if i != n // 2:
                d = i if i < n // 2 else i - 1

                @pl.when(owners[d] == request % n)
                def _(part=part, out=outs[j]):
                    out[...] = part[part.shape[0] - H :, :]


def pick(n, groups, owners, slots, parts):
    return pl.pallas_call(
        functools.partial(pick_kernel, n, groups),
        out_shape=[jax.ShapeDtypeStruct((H, HD), BF16) for _ in range(groups)],
        in_specs=[SMEM, SMEM] + [VMEM] * (n + 1),
        out_specs=[VMEM] * groups,
        compiler_params=params(40),
        cost_estimate=STEP,
        name="pick_queries",
    )(owners, slots, *parts)


def decode_kernel(n, groups, owners, slots, length, cache_in, *rest):
    choices, (out_ref, cache_ref, sems) = rest[:groups], rest[groups:]
    positions = cache_ref.shape[1]
    moving = copies([(cache_in, cache_ref)], sems)
    tok, grp = owners[0], owners[n]
    source = (slots[grp * n + tok] // n) ^ grp
    q = choices[0][...]
    for j in range(1, groups):
        q = jnp.where(source == j, choices[j][...], q)
    head = lax.broadcasted_iota(jnp.int32, (H, positions), 0) // GROUP
    moving[0].wait()
    s = jnp.zeros((H, positions), F32)
    for k in range(KVH):
        one = lax.dot_general(
            q, cache_ref[0, :, k * HD : (k + 1) * HD], (((1,), (1,)), ((), ())), preferred_element_type=F32
        )
        s = jnp.where(head == k, one, s)
    spot = lax.broadcasted_iota(jnp.int32, (H, positions), 1)
    s = jnp.where(spot < length[0], s * (1.0 / math.sqrt(HD)), NEG)
    w = jnp.exp(s - jnp.max(s, axis=-1, keepdims=True)).astype(BF16).astype(F32)
    t = jnp.sum(w, axis=-1, keepdims=True)
    o = jnp.zeros((H, HD), F32)
    for k in range(KVH):
        mine = jnp.where(head == k, w, 0.0).astype(BF16)
        o = o + jnp.dot(
            mine, cache_ref[0, :, WIDTH + k * HD : WIDTH + (k + 1) * HD], preferred_element_type=F32
        )
    out_ref[...] = (o / t).astype(BF16)


def decode(n, owners, slots, length, choices, cache):
    groups = len(choices)
    return pl.pallas_call(
        functools.partial(decode_kernel, n, groups),
        out_shape=jax.ShapeDtypeStruct((H, HD), BF16),
        in_specs=[SMEM, SMEM, SMEM, HBM] + [VMEM] * groups,
        out_specs=VMEM,
        scratch_shapes=[pltpu.VMEM(cache.shape, BF16), pltpu.SemaphoreType.DMA((1,))],
        compiler_params=params(40),
        cost_estimate=STEP,
        name="decode_attention",
    )(owners, slots, length, cache, *choices)


class Fetch:
    def __init__(self, shares=(), blocks=()):
        self.shares, self.blocks = tuple(shares), tuple(blocks)

    def shapes(self, cols, wide):
        out = [jax.ShapeDtypeStruct((len(self.shares) * cols, wide), BF16)] * 2 if self.shares else []
        return out + [jax.ShapeDtypeStruct((wide, cols), BF16) for _ in self.blocks]

    def count(self):
        return 2 * len(self.shares) + len(self.blocks)

    def ins(self):
        return 3 if self.blocks else 2 if self.shares else 0

    def start(self, owners, weights, outs, sems):
        pairs = []
        if self.shares:
            gate, up = weights[:2]
            cols = outs[0].shape[0] // len(self.shares)
            for i, share in enumerate(self.shares):
                at = pl.ds(pl.multiple_of(owners[share] * cols, cols), cols)
                to = pl.ds(i * cols, cols)
                pairs += [(gate.at[at], outs[0].at[to]), (up.at[at], outs[1].at[to])]
            outs = outs[2:]
        for block, out in zip(self.blocks, outs):
            cols = out.shape[1]
            pairs.append((weights[2].at[:, pl.ds(pl.multiple_of(owners[block] * cols, HD), cols)], out))
        return copies(pairs, sems)


def project_kernel(n, rows, fetch, owners, *rest):
    weights, rest = rest[: fetch.ins()], rest[fetch.ins() :]
    parts, (wo_ref, resid_ref, out_ref) = rest[:n], rest[n : n + 3]
    x, dec, sems = rest[-3:]
    moving = fetch.start(owners, weights, rest[n + 3 : -3], sems)
    for d, part in enumerate(parts):
        at = pl.ds(pl.multiple_of(owners[d] * rows, 16), rows)
        for i in range(H):
            x[at, i * HD : (i + 1) * HD] = part[i * rows : (i + 1) * rows, :]
        if part.shape[0] > H * rows:
            dec[pl.ds(pl.multiple_of(owners[d] * H, H), H), :] = part[H * rows :, :]
    spare = x.shape[0] - n * rows
    if spare:
        at = lax.broadcasted_iota(jnp.int32, (H * spare, n * H), 0)
        of = lax.broadcasted_iota(jnp.int32, (H * spare, n * H), 1)
        chosen = jnp.where(of == (at % spare) * H + at // spare, 1.0, 0.0).astype(BF16)
        heads = jnp.dot(chosen, dec[...], preferred_element_type=F32).astype(BF16)
        for i in range(H):
            x[n * rows :, i * HD : (i + 1) * HD] = heads[i * spare : (i + 1) * spare]
    total = jnp.dot(x[...], wo_ref[...], preferred_element_type=F32)
    out_ref[...] = (resid_ref[...].astype(F32) + total).astype(BF16)
    for c in moving:
        c.wait()


def project(rows, owners, parts, wo, resid, fetch, weights):
    m, cols = resid.shape
    n = len(parts)
    fetched = fetch.shapes(cols, weights[0].shape[1])
    return pl.pallas_call(
        functools.partial(project_kernel, n, rows, fetch),
        out_shape=[jax.ShapeDtypeStruct((m, cols), BF16)] + fetched,
        in_specs=[SMEM] + [HBM] * fetch.ins() + [VMEM] * (n + 2),
        out_specs=[VMEM] * (1 + len(fetched)),
        scratch_shapes=[
            pltpu.VMEM((m, D), BF16),
            pltpu.VMEM((n * H, HD), BF16),
            pltpu.SemaphoreType.DMA((max(fetch.count(), 1),)),
        ],
        compiler_params=params(42),
        cost_estimate=STEP,
        name="out_projection",
    )(owners, *weights[: fetch.ins()], *parts, wo, resid)


def scale_in(x, squares, tenants, gain_ref, at):
    for j in range(0, x.shape[1], HD):
        squares = squares + x[:, j : j + HD] * x[:, j : j + HD]
    gain = jnp.broadcast_to(gain_ref[0:1, at], x.shape)
    for t in range(1, gain_ref.shape[0]):
        gain = jnp.where(tenants == t, gain_ref[t : t + 1, at], gain)
    return squares, (x * gain).astype(BF16)


def feed_kernel(shares, taken, fetch, owners, tenants_ref, gain_ref, *rest):
    weights, rest = rest[: fetch.ins()], rest[fetch.ins() :]
    w_refs, rest = rest[:2], rest[2:]
    parts, rest = rest[: 2 * len(shares)], rest[2 * len(shares) :]
    held, rest = (rest[:3], rest[3:]) if taken else (None, rest)
    (gates, lifts, squares), fetched, (scaled, sems) = rest[:3], rest[3:-2], rest[-2:]
    moving = fetch.start(owners, weights, fetched, sems)
    m = gates.shape[0]
    cols = parts[0].shape[1]
    tenants = tenants_ref[...]
    total = held[2][...] if taken else jnp.zeros((m, HD), F32)
    for i, share in enumerate(shares):
        x = jnp.concatenate([p[...] for p in parts[2 * i : 2 * i + 2]], axis=0).astype(F32)
        at = pl.ds(pl.multiple_of(owners[share] * cols, HD), cols)
        total, x = scale_in(x, total, tenants, gain_ref, at)
        scaled[:, i * cols : (i + 1) * cols] = x
    squares[...] = total
    for i, out in enumerate((gates, lifts)):
        one = jnp.dot(scaled[...], w_refs[i][...], preferred_element_type=F32)
        out[...] = held[i][...] + one if taken else one
    for c in moving:
        c.wait()


def feed(shares, owners, tenants, gain, weights, w, parts, held, fetch, grant):
    m, (deep, wide) = tenants.shape[0], w[0].shape
    cols = parts[0].shape[1]
    first = 5 + fetch.ins() + len(parts)
    fetched = fetch.shapes(cols, wide)
    sums = [jax.ShapeDtypeStruct((m, wide), F32)] * 2 + [jax.ShapeDtypeStruct((m, HD), F32)]
    return pl.pallas_call(
        functools.partial(feed_kernel, shares, len(held) > 0, fetch),
        out_shape=sums + fetched,
        in_specs=[SMEM, VMEM, VMEM] + [HBM] * fetch.ins() + [VMEM] * (2 + len(parts) + len(held)),
        out_specs=[VMEM] * (3 + len(fetched)),
        scratch_shapes=[
            pltpu.VMEM((m, deep), BF16),
            pltpu.SemaphoreType.DMA((fetch.count(),)),
        ],
        input_output_aliases={first + i: i for i in range(len(held))},
        compiler_params=params(grant),
        cost_estimate=STEP,
        name="gate_up_sum",
    )(owners, tenants, gain, *weights[: fetch.ins()], *w, *parts, *held)


def hidden_kernel(lo, hi, share, owners, tenants_ref, gain_ref, w_gate, w_up, part, gates, lifts, squares, out):
    cols = part.shape[1]
    at = pl.ds(pl.multiple_of(owners[share] * cols, HD), cols)
    total, x = scale_in(part[...].astype(F32), squares[lo:hi, :], tenants_ref[lo:hi, :], gain_ref, at)
    scale = lax.rsqrt(jnp.sum(total, axis=-1, keepdims=True) / D + EPS)
    gate = (gates[lo:hi, :] + jnp.dot(x, w_gate[...], preferred_element_type=F32)) * scale
    gate = gate / (1.0 + jnp.exp(-gate))
    lift = (lifts[lo:hi, :] + jnp.dot(x, w_up[...], preferred_element_type=F32)) * scale
    out[...] = (gate * lift).astype(BF16)


def hide(lo, hi, share, owners, tenants, gain, w, part, held):
    return pl.pallas_call(
        functools.partial(hidden_kernel, lo, hi, share),
        out_shape=jax.ShapeDtypeStruct((hi - lo, w[0].shape[1]), BF16),
        in_specs=[SMEM] + [VMEM] * 8,
        out_specs=VMEM,
        compiler_params=params(16),
        cost_estimate=STEP,
        name="hidden",
    )(owners, tenants, gain, *w, part, *held)


def down_kernel(flags, own, owners, hidden, *rest):
    count = len(flags)
    weights, rest = rest[:count], rest[count:]
    terms, outs = rest[: sum(flags) + own], rest[sum(flags) + own :]
    taken = 0
    for i in range(count):
        total = jnp.dot(hidden[...], weights[i][...], preferred_element_type=F32)
        for term in terms[taken : taken + flags[i] + own]:
            total = total + term[...].astype(F32)
        taken += flags[i]
        outs[i][...] = total.astype(BF16)


def down(flags, owners, hidden, weights, arrived, own=()):
    m, cols = hidden.shape[0], weights[0].shape[1]
    return pl.pallas_call(
        functools.partial(down_kernel, flags, len(own)),
        out_shape=[jax.ShapeDtypeStruct((m, cols), BF16) for _ in flags],
        in_specs=[SMEM] + [VMEM] * (1 + len(flags) + len(arrived) + len(own)),
        out_specs=[VMEM] * len(flags),
        compiler_params=params(16),
        cost_estimate=STEP,
        name="down_sum",
    )(owners, hidden, *weights, *arrived, *own)


class Chain:
    def __init__(self, n, order, own, last, cut=0):
        self.n, self.half, self.last, self.cut = n, n // 2, last, cut
        self.fw = [(order[i], order[(i + 1) % n]) for i in range(n)]
        self.bw = [(b, a) for a, b in self.fw]
        self.own, self.ahead, self.behind, self.hops = own, [own], [own], 0

    def done(self):
        return self.hops == self.half

    def parts(self):
        return [self.own] + self.ahead[1:] + self.behind[:0:-1]


class Order:
    def __init__(self, ids):
        self.ids, self.last = ids, ()

    def after(self):
        return lax.optimization_barrier((self.ids, *self.last))[0]

    def mark(self, *out):
        self.last = out
        return out[0]

    def tied(self, *arrays):
        out = lax.optimization_barrier((*arrays, *self.last))[: len(arrays)]
        self.last = (out[0],)
        return out

    def hop(self, chain):
        chain.hops += 1
        f, b = chain.ahead[-1], chain.behind[-1]
        if chain.done() and chain.last == "split":
            f, b = f[: chain.cut], b[chain.cut :]
        if chain.done() and chain.last == "fw":
            (f,) = self.tied(f)
            chain.ahead.append(lax.ppermute(f, "tok", chain.fw))
        elif chain.done() and chain.last == "bw":
            (b,) = self.tied(b)
            chain.behind.append(lax.ppermute(b, "tok", chain.bw))
        else:
            f, b = self.tied(f, b)
            chain.ahead.append(lax.ppermute(f, "tok", chain.fw))
            chain.behind.append(lax.ppermute(b, "tok", chain.bw))


class Sum:
    def __init__(self, run, chain, hidden, blocks, own):
        self.run, self.chain, self.hidden, self.blocks = run, chain, hidden, blocks
        self.own, self.step, self.arrived = own, 0, ()

    def call(self, blocks, flags, own=()):
        weights = [self.blocks[-b % self.chain.n] for b in blocks]
        out = down(flags, self.run.after(), self.hidden, weights, self.arrived, own)
        self.run.mark(out[0])
        return out

    def hop(self):
        chain = self.chain
        d, forward = chain.half - self.step, chain.last == "fw"
        if self.step == 0:
            out = self.run.tied(*self.call([d], [0]))
            self.arrived = (lax.ppermute(out[0], "tok", chain.fw if forward else chain.bw),)
        else:
            flags = [1, 1] if self.step > 1 else ([1, 0] if forward else [0, 1])
            out = self.run.tied(*self.call([d, -d], flags))
            self.arrived = (lax.ppermute(out[0], "tok", chain.fw), lax.ppermute(out[1], "tok", chain.bw))
        self.step += 1

    def finish(self):
        return self.call([0], [2], (self.own,))[0]


def shards(
    pre_q,
    pre_kv,
    pre_segment,
    dec_q,
    cache,
    cache_len,
    slot_request,
    resid,
    wo,
    tenant,
    norm_gain,
    w_gate,
    w_up,
    w_down,
):
    n, groups = lax.axis_size("tok"), lax.axis_size("grp")
    tok, grp = lax.axis_index("tok"), lax.axis_index("grp")
    local = pre_q.shape[0]
    rows = local // 2
    cols = wo.shape[1]
    half = n // 2
    spare = -(-n // 16) * 16
    order = ring_order(n)
    ids = jnp.arange(n, dtype=jnp.int32)
    place = sum(jnp.where(tok == t, i, 0) for i, t in enumerate(order)).astype(jnp.int32)
    spots = (place - ids) % n
    owners = sum(jnp.where(spots == i, t, 0) for i, t in enumerate(order)).astype(jnp.int32)
    owners = jnp.concatenate([owners, jnp.reshape(grp, (1,)).astype(jnp.int32)])

    def split(a):
        a = a.reshape(n, local + 1, -1)
        first = a[:, :rows].reshape(n * rows, -1)
        second = a[:, rows:local].reshape(n * rows, -1)
        tail = jnp.pad(a[:, local], ((0, spare - n), (0, 0)))
        return first, jnp.concatenate([second, tail], axis=0)

    resids = split(resid)
    tenants = jnp.concatenate(split(tenant[0][:, None]), axis=0)
    run = Order(owners)

    def chain(own, last):
        return Chain(n, order, own, last)

    keys = Chain(n, order, pack(pre_kv, dec_q), "split", KVH * local)
    run.hop(keys)
    run.mark(*run.last, *resids, tenants, owners)
    while not keys.done():
        run.hop(keys)
    kv = keys.parts()
    a = chain(run.mark(attention(0, rows, run.after(), pre_q, pre_segment, kv)), "fw")
    run.hop(a)
    choices = list(pick(n, groups, run.after(), slot_request, kv))
    run.mark(choices[0])
    for j in range(1, groups):
        (choices[j],) = run.tied(choices[j])
        choices[j] = lax.ppermute(choices[j], "grp", [(i, i ^ j) for i in range(groups)])
    run.hop(a)
    dec = run.mark(decode(n, run.after(), slot_request, cache_len, choices, cache))
    b = chain(run.mark(attention(rows, rows, run.after(), pre_q, pre_segment, kv, (dec,))), "bw")
    run.hop(b)
    while not a.done():
        run.hop(a)
        run.hop(b)

    weights = (w_gate, w_up, w_down)
    mixed_a = project(rows, run.after(), a.parts(), wo, resids[0], Fetch(), weights)[0]
    run.mark(mixed_a)
    g = chain(mixed_a, "fw")
    run.hop(g)
    while not b.done():
        run.hop(b)
        if not b.done():
            run.hop(g)
    mixed_b, *w = project(rows, run.after(), b.parts(), wo, resids[1], Fetch([0]), weights)
    run.mark(mixed_b)
    h = chain(mixed_b, "bw")
    run.hop(h)

    m_a, m = mixed_a.shape[0], tenants.shape[0]
    held, blocks = (), {}
    for i in range(half):
        shares = [i, n - i] if i else [0]
        if i:
            parts = [g.ahead[i], h.ahead[i], g.behind[i], h.behind[i]]
        else:
            parts = [mixed_a, mixed_b]
        later = [half] if i + 1 == half else [i + 1, n - i - 1]
        early = []
        if i == 1:
            early = [half]
        elif i > 1:
            early = [half + 1 - i, n - half - 1 + i]
        if i + 1 == half:
            early += [d for d in range(n) if d not in early and d not in blocks]
        grant = 30 if i == 0 else 20 if i + 1 == half else 24
        out = feed(
            shares, run.after(), tenants, norm_gain, weights, w, parts, held, Fetch(later, early), grant
        )
        held, w = out[:3], out[3:5]
        blocks.update(zip(early, out[5:]))
        run.mark(out[2])
        if not g.done():
            run.hop(g)
        if not h.done():
            run.hop(h)

    def finish(lo, hi, part):
        return run.mark(hide(lo, hi, half, run.after(), tenants, norm_gain, w, part, held))

    hid_a = finish(0, m_a, g.ahead[half])
    sum_a = Sum(run, g, hid_a, blocks, mixed_a)
    sum_a.hop()
    hid_b = finish(m_a, m, h.behind[half])
    sum_b = Sum(run, h, hid_b, blocks, mixed_b)
    sum_b.hop()
    for _ in range(1, half):
        sum_a.hop()
        sum_b.hop()
    out_a = sum_a.finish()
    out_b = sum_b.finish()

    top = out_a.reshape(n, rows, cols)
    low = out_b[: n * rows].reshape(n, rows, cols)
    tail = out_b[n * rows : n * rows + n].reshape(n, 1, cols)
    return jnp.concatenate([top, low, tail], axis=1).reshape(n * (local + 1), cols)


def solution(mesh):
    in_specs = (
        P(("grp", "tok"), None),
        P(("grp", "tok"), None),
        P("grp", None),
        P(("grp", "tok"), None),
        P(("grp", "tok"), None, None),
        P(("grp", "tok")),
        P(),
        P("grp", "tok"),
        P(None, "tok"),
        P("grp", None),
        P(),
        P(None, "tok"),
        P(None, "tok"),
        P("tok", None),
    )
    out_specs = P("grp", "tok")
    return jax.shard_map(shards, mesh=mesh, in_specs=in_specs, out_specs=out_specs, check_vma=False)
```

```python
import functools
import math

import jax
import jax.numpy as jnp
from jax import lax
from jax.experimental import pallas as pl
from jax.experimental.pallas import tpu as pltpu
from jax.sharding import PartitionSpec as P

D = 4096
H = 32
KVH = 8
HD = 128
GROUP = H // KVH
WIDTH = KVH * HD
EPS = 1e-05
NEG = -1e30
Z_CHIPS = 4

HBM = pl.BlockSpec(memory_space=pltpu.HBM)
VMEM = pl.BlockSpec(memory_space=pltpu.VMEM)
SMEM = pl.BlockSpec(memory_space=pltpu.SMEM)
F32 = jnp.float32
BF16 = jnp.bfloat16


def ring_order(n):
    columns = n // Z_CHIPS
    if n % Z_CHIPS or columns % 2:
        return list(range(n))
    order = [z * columns for z in range(Z_CHIPS)]
    for i, z in enumerate(reversed(range(Z_CHIPS))):
        xs = range(1, columns) if i % 2 == 0 else range(columns - 1, 0, -1)
        order += [z * columns + x for x in xs]
    return order


def params(mib):
    return pltpu.CompilerParams(vmem_limit_bytes=mib * 2**20)


STEP = pl.CostEstimate(flops=500_000_000, bytes_accessed=1_000_000, transcendentals=0)


def copies(pairs, sems):
    out = [pltpu.make_async_copy(src, dst, sems.at[i]) for i, (src, dst) in enumerate(pairs)]
    for c in out:
        c.start()
    return out


def in_hbm(x):
    return pltpu.with_memory_space_constraint(x, pltpu.HBM)


def pack_kernel(kv_ref, ask_ref, keys_ref, values_ref):
    rows = kv_ref.shape[0]
    for i in range(KVH):
        keys_ref[i * rows : (i + 1) * rows, :] = kv_ref[:, i * HD : (i + 1) * HD]
        values_ref[i * rows : (i + 1) * rows, :] = kv_ref[:, WIDTH + i * HD : WIDTH + (i + 1) * HD]
    ask = ask_ref[...].astype(F32)
    heads = jnp.concatenate([ask[:, i * HD : (i + 1) * HD] for i in range(H)], axis=0)
    keys_ref[KVH * rows :, :] = heads.astype(BF16)


def pack(kv, ask):
    rows = kv.shape[0]
    return pl.pallas_call(
        pack_kernel,
        out_shape=[
            jax.ShapeDtypeStruct((KVH * rows + H, HD), BF16),
            jax.ShapeDtypeStruct((KVH * rows, HD), BF16),
        ],
        in_specs=[VMEM, VMEM],
        out_specs=[VMEM, VMEM],
        cost_estimate=STEP,
        name="pack_keys",
    )(kv, ask)


def attention_kernel(count, first, rows, owners, q_in, seg_ref, *rest):
    parts, (out_ref, kv, q, sems) = rest[:count], rest[-4:]
    total = kv.shape[1]
    local = q_in.shape[0]
    moving = copies([(q_in.at[pl.ds(first, rows)], q)], sems)
    for j, part in enumerate(parts):
        at = pl.ds(pl.multiple_of(owners[j % (count // 2)] * local, 16), local)
        for i in range(KVH):
            kv[j // (count // 2) * KVH + i, at, :] = part[i * local : (i + 1) * local, :]
    key_pos = lax.broadcasted_iota(jnp.int32, (rows, total), 1)
    query_pos = lax.broadcasted_iota(jnp.int32, (rows, total), 0) + (owners[0] * local + first)
    span = jnp.broadcast_to(seg_ref[...], (rows, total)).astype(F32)
    own_span = jnp.sum(jnp.where(key_pos == query_pos, span, 0.0), axis=-1, keepdims=True)
    seen = (key_pos <= query_pos) & (span == own_span)
    bias = jnp.where(seen, 0.0, NEG).astype(F32)
    bias = jnp.concatenate([bias] * GROUP, axis=0)
    if len(rest) > count + 4:
        out_ref[H * rows :, :] = rest[count][...]
    moving[0].wait()
    for k in range(KVH):
        heads = range(k * GROUP, (k + 1) * GROUP)
        four = jnp.concatenate([q[:, i * HD : (i + 1) * HD] for i in heads], axis=0)
        s = lax.dot_general(four, kv[k], (((1,), (1,)), ((), ())), preferred_element_type=F32)
        s = s * (1.0 / math.sqrt(HD)) + bias
        w = jnp.exp(s - jnp.max(s, axis=-1, keepdims=True)).astype(BF16)
        t = jnp.sum(w.astype(F32), axis=-1, keepdims=True)
        o = jnp.dot(w, kv[KVH + k], preferred_element_type=F32) / t
        out_ref[k * GROUP * rows : (k + 1) * GROUP * rows, :] = o.astype(BF16)


def attention(first, rows, owners, q, seg, parts, dec=()):
    total = seg.shape[1]
    return pl.pallas_call(
        functools.partial(attention_kernel, len(parts), first, rows),
        out_shape=jax.ShapeDtypeStruct((H * (rows + len(dec)), HD), BF16),
        in_specs=[SMEM, HBM, VMEM] + [VMEM] * (len(parts) + len(dec)),
        out_specs=VMEM,
        scratch_shapes=[
            pltpu.VMEM((2 * KVH, total, HD), BF16),
            pltpu.VMEM((rows, D), BF16),
            pltpu.SemaphoreType.DMA((1,)),
        ],
        compiler_params=params(16),
        cost_estimate=STEP,
        name="prefill_attention",
    )(owners, q, seg, *parts, *dec)


def pick_kernel(n, groups, owners, slots, *rest):
    parts, outs = rest[:n], rest[n:]
    tok, grp = owners[0], owners[n]
    for j in range(groups):
        request = slots[(grp ^ j) * n + tok]
        for d, part in enumerate(parts):

            @pl.when(owners[d] == request % n)
            def _(part=part, out=outs[j]):
                out[...] = part[part.shape[0] - H :, :]


def pick(n, groups, owners, slots, parts):
    return pl.pallas_call(
        functools.partial(pick_kernel, n, groups),
        out_shape=[jax.ShapeDtypeStruct((H, HD), BF16) for _ in range(groups)],
        in_specs=[SMEM, SMEM] + [VMEM] * n,
        out_specs=[VMEM] * groups,
        compiler_params=params(16),
        cost_estimate=STEP,
        name="pick_queries",
    )(owners, slots, *parts)


def decode_kernel(n, groups, owners, slots, length, cache_in, *rest):
    choices, (out_ref, cache_ref, sems) = rest[:groups], rest[groups:]
    positions = cache_ref.shape[1]
    moving = copies([(cache_in, cache_ref)], sems)
    tok, grp = owners[0], owners[n]
    source = (slots[grp * n + tok] // n) ^ grp
    q = choices[0][...]
    for j in range(1, groups):
        q = jnp.where(source == j, choices[j][...], q)
    head = lax.broadcasted_iota(jnp.int32, (H, positions), 0) // GROUP
    moving[0].wait()
    s = jnp.zeros((H, positions), F32)
    for k in range(KVH):
        one = lax.dot_general(
            q, cache_ref[0, :, k * HD : (k + 1) * HD], (((1,), (1,)), ((), ())), preferred_element_type=F32
        )
        s = jnp.where(head == k, one, s)
    spot = lax.broadcasted_iota(jnp.int32, (H, positions), 1)
    s = jnp.where(spot < length[0], s * (1.0 / math.sqrt(HD)), NEG)
    w = jnp.exp(s - jnp.max(s, axis=-1, keepdims=True)).astype(BF16).astype(F32)
    t = jnp.sum(w, axis=-1, keepdims=True)
    o = jnp.zeros((H, HD), F32)
    for k in range(KVH):
        mine = jnp.where(head == k, w, 0.0).astype(BF16)
        o = o + jnp.dot(
            mine, cache_ref[0, :, WIDTH + k * HD : WIDTH + (k + 1) * HD], preferred_element_type=F32
        )
    out_ref[...] = (o / t).astype(BF16)


def decode(n, owners, slots, length, choices, cache):
    groups = len(choices)
    return pl.pallas_call(
        functools.partial(decode_kernel, n, groups),
        out_shape=jax.ShapeDtypeStruct((H, HD), BF16),
        in_specs=[SMEM, SMEM, SMEM, HBM] + [VMEM] * groups,
        out_specs=VMEM,
        scratch_shapes=[pltpu.VMEM(cache.shape, BF16), pltpu.SemaphoreType.DMA((1,))],
        compiler_params=params(16),
        cost_estimate=STEP,
        name="decode_attention",
    )(owners, slots, length, cache, *choices)


class Fetch:
    def __init__(self, shares=(), blocks=()):
        self.shares, self.blocks = tuple(shares), tuple(blocks)

    def shapes(self, cols, wide):
        out = [pltpu.VMEM((cols, wide), BF16)] * (2 * len(self.shares))
        return out + [pltpu.VMEM((wide, cols), BF16) for _ in self.blocks]

    def count(self):
        return 2 * len(self.shares) + len(self.blocks)

    def outs(self):
        return 2 * len(self.shares) + len(self.blocks)

    def ins(self):
        return 3 if self.blocks else 2 if self.shares else 0

    def start(self, owners, weights, outs, sems):
        pairs = []
        if self.shares:
            gate, up = weights[:2]
            cols = outs[0].shape[0]
            for share in self.shares:
                at = pl.ds(pl.multiple_of(owners[share] * cols, cols), cols)
                pairs += [(gate.at[at], outs[0]), (up.at[at], outs[1])]
                outs = outs[2:]
        for block, out in zip(self.blocks, outs):
            cols = out.shape[1]
            pairs.append((weights[2].at[:, pl.ds(pl.multiple_of(owners[block] * cols, HD), cols)], out))
        return copies(pairs, sems)


def fetch_kernel(fetch, owners, *rest):
    for c in fetch.start(owners, rest[: fetch.ins()], rest[fetch.ins() : -1], rest[-1]):
        c.wait()


def fetch_early(fetch, owners, weights, cols, wide):
    shapes = fetch.shapes(cols, wide)
    return pl.pallas_call(
        functools.partial(fetch_kernel, fetch),
        out_shape=shapes,
        in_specs=[SMEM] + [HBM] * fetch.ins(),
        out_specs=[VMEM] * len(shapes),
        scratch_shapes=[pltpu.SemaphoreType.DMA((fetch.count(),))],
        compiler_params=params(16),
        cost_estimate=STEP,
        name="fetch_weights",
    )(owners, *[in_hbm(x) for x in weights[: fetch.ins()]])


def project_kernel(n, rows, first, owners, *rest):
    parts, (wo_ref, resid_ref, out_ref, x, dec, resid) = rest[:n], rest[n:]
    resid[...] = resid_ref[...].astype(F32)
    local = resid.shape[0] // n
    wide = [resid[b * local + first : b * local + first + rows, :] for b in range(n)]
    for d, part in enumerate(parts):
        at = pl.ds(pl.multiple_of(owners[d] * rows, 16), rows)
        for i in range(H):
            x[at, i * HD : (i + 1) * HD] = part[i * rows : (i + 1) * rows, :]
        if part.shape[0] > H * rows:
            dec[pl.ds(pl.multiple_of(owners[d] * H, H), H), :] = part[H * rows :, :]
    spare = x.shape[0] - n * rows
    if spare:
        at = lax.broadcasted_iota(jnp.int32, (H * spare, n * H), 0)
        of = lax.broadcasted_iota(jnp.int32, (H * spare, n * H), 1)
        chosen = jnp.where(of == (at % spare) * H + at // spare, 1.0, 0.0).astype(BF16)
        heads = jnp.dot(chosen, dec[...], preferred_element_type=F32).astype(BF16)
        for i in range(H):
            x[n * rows :, i * HD : (i + 1) * HD] = heads[i * spare : (i + 1) * spare]
        wide += [resid[(b + 1) * local - 1 : (b + 1) * local, :] for b in range(n)]
        if spare > n:
            wide.append(jnp.zeros((spare - n, resid.shape[1]), F32))
    total = jnp.dot(x[...], wo_ref[...], preferred_element_type=F32)
    out_ref[...] = (jnp.concatenate(wide, axis=0) + total).astype(BF16)


def project(rows, spare, first, owners, parts, wo, resid):
    n = len(parts)
    m, cols = n * rows + spare, wo.shape[1]
    return pl.pallas_call(
        functools.partial(project_kernel, n, rows, first),
        out_shape=jax.ShapeDtypeStruct((m, cols), BF16),
        in_specs=[SMEM] + [VMEM] * (n + 2),
        out_specs=VMEM,
        scratch_shapes=[
            pltpu.VMEM((m, D), BF16),
            pltpu.VMEM((n * H, HD), BF16),
            pltpu.VMEM(resid.shape, F32),
        ],
        compiler_params=params(16),
        cost_estimate=STEP,
        name="out_projection",
    )(owners, *parts, wo, resid)


def scale_in(x, squares, tenants, gain_ref, at):
    for j in range(0, x.shape[1], HD):
        squares = squares + x[:, j : j + HD] * x[:, j : j + HD]
    gain = jnp.broadcast_to(gain_ref[0:1, at], x.shape)
    for t in range(1, gain_ref.shape[0]):
        gain = jnp.where(tenants == t, gain_ref[t : t + 1, at], gain)
    return squares, (x * gain).astype(BF16)


def feed_kernel(lo, hi, shares, taken, fetch, owners, tenants_ref, gain_ref, *rest):
    weights, rest = rest[: fetch.ins()], rest[fetch.ins() :]
    w_refs, rest = rest[: 2 * len(shares)], rest[2 * len(shares) :]
    chunks = (len(rest) - 5 - fetch.outs() - 3 * taken) // len(shares)
    parts, rest = rest[: chunks * len(shares)], rest[chunks * len(shares) :]
    held, rest = (rest[:3], rest[3:]) if taken else (None, rest)
    (gates, lifts, squares), fetched, (scaled, sems) = rest[:3], rest[3:-2], rest[-2:]
    moving = fetch.start(owners, weights, fetched, sems)
    cols = parts[0].shape[1]
    tenants = tenants_ref[lo:hi, :]
    total = held[2][lo:hi, :] if taken else jnp.zeros((hi - lo, HD), F32)
    for i, share in enumerate(shares):
        x = jnp.concatenate([p[...] for p in parts[chunks * i : chunks * (i + 1)]], axis=0).astype(F32)
        at = pl.ds(pl.multiple_of(owners[share] * cols, HD), cols)
        total, x = scale_in(x, total, tenants, gain_ref, at)
        scaled[:, i * cols : (i + 1) * cols] = x
    squares[lo:hi, :] = total
    for i, out in enumerate((gates, lifts)):
        one = jnp.dot(scaled[:, :cols], w_refs[i][...], preferred_element_type=F32)
        if len(shares) > 1:
            one = one + jnp.dot(scaled[:, cols:], w_refs[2 + i][...], preferred_element_type=F32)
        out[lo:hi, :] = held[i][lo:hi, :] + one if taken else one
    for c in moving:
        c.wait()


def feed(lo, hi, shares, owners, tenants, gain, weights, w, parts, held, fetch, grant):
    m, wide = tenants.shape[0], w[0].shape[1]
    cols = parts[0].shape[1]
    first = 3 + fetch.ins() + len(w) + len(parts)
    fetched = fetch.shapes(cols, wide)
    sums = [jax.ShapeDtypeStruct((m, wide), F32)] * 2 + [jax.ShapeDtypeStruct((m, HD), F32)]
    return pl.pallas_call(
        functools.partial(feed_kernel, lo, hi, shares, len(held) > 0, fetch),
        out_shape=sums + fetched,
        in_specs=[SMEM, VMEM, VMEM] + [HBM] * fetch.ins() + [VMEM] * (len(w) + len(parts) + len(held)),
        out_specs=[VMEM] * (3 + len(fetched)),
        scratch_shapes=[
            pltpu.VMEM((hi - lo, cols * len(shares)), BF16),
            pltpu.SemaphoreType.DMA((max(fetch.count(), 1),)),
        ],
        input_output_aliases={first + i: i for i in range(len(held))},
        compiler_params=params(16),
        cost_estimate=STEP,
        name="gate_up_sum",
    )(owners, tenants, gain, *[in_hbm(x) for x in weights[: fetch.ins()]], *w, *parts, *held)


def hidden_kernel(lo, hi, share, owners, tenants_ref, gain_ref, w_gate, w_up, part, gates, lifts, squares, out):
    cols = part.shape[1]
    at = pl.ds(pl.multiple_of(owners[share] * cols, HD), cols)
    total, x = scale_in(part[...].astype(F32), squares[lo:hi, :], tenants_ref[lo:hi, :], gain_ref, at)
    scale = lax.rsqrt(jnp.sum(total, axis=-1, keepdims=True) / D + EPS)
    gate = (gates[lo:hi, :] + jnp.dot(x, w_gate[...], preferred_element_type=F32)) * scale
    gate = gate / (1.0 + jnp.exp(-gate))
    lift = (lifts[lo:hi, :] + jnp.dot(x, w_up[...], preferred_element_type=F32)) * scale
    out[...] = (gate * lift).astype(BF16)


def hide(lo, hi, share, owners, tenants, gain, w, part, held):
    return pl.pallas_call(
        functools.partial(hidden_kernel, lo, hi, share),
        out_shape=jax.ShapeDtypeStruct((hi - lo, w[0].shape[1]), BF16),
        in_specs=[SMEM] + [VMEM] * 8,
        out_specs=VMEM,
        compiler_params=params(16),
        cost_estimate=STEP,
        name="hidden",
    )(owners, tenants, gain, *w, part, *held)


def down_kernel(flags, own, owners, hidden, *rest):
    count = len(flags)
    weights, rest = rest[:count], rest[count:]
    terms, outs = rest[: sum(flags) + own], rest[sum(flags) + own :]
    taken = 0
    for i in range(count):
        total = jnp.dot(hidden[...], weights[i][...], preferred_element_type=F32)
        for term in terms[taken : taken + flags[i] + own]:
            total = total + term[...].astype(F32)
        taken += flags[i]
        outs[i][...] = total.astype(BF16)


def down(flags, owners, hidden, weights, arrived, own=()):
    m, cols = hidden.shape[0], weights[0].shape[1]
    return pl.pallas_call(
        functools.partial(down_kernel, flags, len(own)),
        out_shape=[jax.ShapeDtypeStruct((m, cols), BF16) for _ in flags],
        in_specs=[SMEM] + [VMEM] * (1 + len(flags) + len(arrived) + len(own)),
        out_specs=[VMEM] * len(flags),
        compiler_params=params(16),
        cost_estimate=STEP,
        name="down_sum",
    )(owners, hidden, *weights, *arrived, *own)


class Chain:
    def __init__(self, n, order, own, last):
        self.n, self.half, self.last = n, n // 2, last
        self.fw = [(order[i], order[(i + 1) % n]) for i in range(n)]
        self.bw = [(b, a) for a, b in self.fw]
        self.own, self.ahead, self.behind, self.hops = own, [own], [own], 0

    def done(self):
        return self.hops == self.half

    def parts(self):
        return [self.own] + self.ahead[1:] + self.behind[:0:-1]


def settle_kernel(*refs):
    for i in range(len(refs) // 2):
        refs[len(refs) // 2 + i][...] = refs[i][...]


def settle(*arrays):
    return pl.pallas_call(
        settle_kernel,
        out_shape=[jax.ShapeDtypeStruct(x.shape, x.dtype) for x in arrays],
        in_specs=[VMEM] * len(arrays),
        out_specs=[VMEM] * len(arrays),
        cost_estimate=STEP,
        name="settle",
    )(*arrays)


def tick_kernel(token, out):
    out[...] = token[...]


def tick(token):
    return pl.pallas_call(
        tick_kernel,
        out_shape=jax.ShapeDtypeStruct(token.shape, token.dtype),
        in_specs=[VMEM],
        out_specs=VMEM,
        cost_estimate=STEP,
        name="tick",
    )(token)


class Order:
    def __init__(self, ids):
        self.ids, self.last = ids, ()
        self.token = jnp.zeros((8, HD), F32)

    def after(self):
        return lax.optimization_barrier((self.ids, *self.last))[0]

    def mark(self, *out):
        self.last = out
        return out[0]

    def tick(self):
        self.token = tick(lax.optimization_barrier((self.token, *self.last))[0])

    def tied(self, *arrays):
        out = lax.optimization_barrier((*arrays, self.token, *self.last))
        self.last, self.token = (out[0],), out[len(arrays)]
        return out[: len(arrays)]

    def hop(self, chain):
        chain.hops += 1
        f, b = chain.ahead[-1], chain.behind[-1]
        f, b = self.tied(f, b)
        if chain.done() and chain.last == "fw":
            chain.ahead.append(lax.ppermute(f, "tok", chain.fw))
        elif chain.done():
            chain.behind.append(lax.ppermute(b, "tok", chain.bw))
        else:
            chain.ahead.append(lax.ppermute(f, "tok", chain.fw))
            chain.behind.append(lax.ppermute(b, "tok", chain.bw))


class Sum:
    def __init__(self, run, chain, hidden, blocks, own):
        self.run, self.chain, self.hidden, self.blocks = run, chain, hidden, blocks
        self.own, self.step, self.arrived = own, 0, ()

    def call(self, blocks, flags, own=()):
        weights = [self.blocks[-b % self.chain.n] for b in blocks]
        out = down(flags, self.run.after(), self.hidden, weights, self.arrived, own)
        self.run.mark(out[0])
        return out

    def hop(self):
        chain = self.chain
        d, forward = chain.half - self.step, chain.last == "fw"
        if self.step == 0:
            out = self.run.tied(*self.call([d], [0]))
            self.arrived = (lax.ppermute(out[0], "tok", chain.fw if forward else chain.bw),)
        else:
            flags = [1, 1] if self.step > 1 else ([1, 0] if forward else [0, 1])
            out = self.run.tied(*self.call([d, -d], flags))
            self.arrived = (lax.ppermute(out[0], "tok", chain.fw), lax.ppermute(out[1], "tok", chain.bw))
        self.step += 1

    def finish(self):
        return self.call([0], [2], (self.own,))[0]


def shards(
    pre_q,
    pre_kv,
    pre_segment,
    dec_q,
    cache,
    cache_len,
    slot_request,
    resid,
    wo,
    tenant,
    norm_gain,
    w_gate,
    w_up,
    w_down,
):
    n, groups = lax.axis_size("tok"), lax.axis_size("grp")
    tok, grp = lax.axis_index("tok"), lax.axis_index("grp")
    local = pre_q.shape[0]
    rows = local // 2
    cols = wo.shape[1]
    half = n // 2
    spare = -(-n // 16) * 16
    order = ring_order(n)
    ids = jnp.arange(n, dtype=jnp.int32)
    place = sum(jnp.where(tok == t, i, 0) for i, t in enumerate(order)).astype(jnp.int32)
    spots = (place - ids) % n
    owners = sum(jnp.where(spots == i, t, 0) for i, t in enumerate(order)).astype(jnp.int32)
    owners = jnp.concatenate([owners, jnp.reshape(grp, (1,)).astype(jnp.int32)])

    def split(a):
        a = a.reshape(n, local + 1, -1)
        first = a[:, :rows].reshape(n * rows, -1)
        second = a[:, rows:local].reshape(n * rows, -1)
        tail = jnp.pad(a[:, local], ((0, spare - n), (0, 0)))
        return first, jnp.concatenate([second, tail], axis=0)

    tenants = jnp.concatenate(split(tenant[0][:, None]), axis=0)
    run = Order(owners)

    def chain(own, last):
        return Chain(n, order, own, last)

    own_keys, own_values = pack(pre_kv, dec_q)
    keys, values = chain(own_keys, "fw"), chain(own_values, "bw")
    run.hop(keys)
    run.tick()
    run.hop(values)
    while not keys.done():
        run.tick()
        run.hop(keys)
        run.tick()
        run.hop(values)
    choices = list(pick(n, groups, run.after(), slot_request, keys.parts()))
    run.mark(choices[0])
    for j in range(1, groups):
        (choices[j],) = run.tied(choices[j])
        choices[j] = lax.ppermute(choices[j], "grp", [(i, i ^ j) for i in range(groups)])
    kv = keys.parts() + values.parts()
    a = chain(run.mark(attention(0, rows, run.after(), pre_q, pre_segment, kv)), "fw")
    run.hop(a)
    dec = run.mark(decode(n, run.after(), slot_request, cache_len, choices, cache))
    b = chain(run.mark(attention(rows, rows, run.after(), pre_q, pre_segment, kv, (dec,))), "bw")
    run.hop(b)
    run.hop(a)
    tenants, gain = settle(tenants, norm_gain)
    run.mark(*run.last, tenants)
    run.hop(b)
    weights = (w_gate, w_up, w_down)
    wide = w_gate.shape[1]
    far = [d for d in range(half - 1, half + 2)]
    fetches = [Fetch([0]), Fetch([1]), Fetch([n - 1]), Fetch((), far)]
    blocks, early = {}, {}

    def fetch_some():
        if fetches:
            fetch = fetches.pop(0)
            out = fetch_early(fetch, run.after(), weights, cols, wide)
            run.mark(out[0])
            blocks.update(zip(fetch.blocks, out))
            early.update({share: out for share in fetch.shares})

    while not a.done():
        run.hop(a)
        fetch_some()
        run.hop(b)
        fetch_some()
    while fetches:
        fetch_some()
    mixed_a = run.mark(project(rows, 0, 0, run.after(), a.parts(), wo, resid))
    g = chain(mixed_a, "fw")
    run.hop(g)
    mixed_b = run.mark(project(rows, spare, rows, run.after(), b.parts(), wo, resid))
    h = chain(mixed_b, "bw")
    run.hop(h)

    m_a, m = mixed_a.shape[0], tenants.shape[0]
    held = ()

    def add(lo, hi, shares, parts, fetch, grant):
        w = [x for share in shares for x in early[share]]
        out = feed(lo, hi, shares, run.after(), tenants, gain, weights, w, parts, held, fetch, grant)
        run.mark(out[2])
        for i, share in enumerate(fetch.shares):
            early[share] = out[3 + 2 * i : 5 + 2 * i]
        blocks.update(zip(fetch.blocks, out[3 + 2 * len(fetch.shares) :]))
        return out[:3]

    def arrived(i):
        return [g.ahead[i], h.ahead[i], g.behind[i], h.behind[i]]

    held = add(0, m, [0], [mixed_a, mixed_b], Fetch([2, n - 2] if half > 2 else [half]), 24)
    run.hop(g)
    run.hop(h)
    for i in range(1, half - 1):
        if i == 1:
            fetch = Fetch((), [half - 2, half + 2])
        else:
            fetch = Fetch([i + 1, n - i - 1])
        held = add(0, m, [i, n - i], arrived(i), fetch, 24)
        run.hop(g)
        run.hop(h)
    i = half - 1
    held = add(0, m_a, [i, n - i], arrived(i)[::2], Fetch([half], [d for d in range(1, n) if d not in blocks]), 16)

    def finish(lo, hi, part):
        return run.mark(hide(lo, hi, half, run.after(), tenants, gain, early[half], part, held))

    hid_a = finish(0, m_a, g.ahead[half])
    sum_a = Sum(run, g, hid_a, blocks, mixed_a)
    sum_a.hop()
    held = add(m_a, m, [i, n - i], arrived(i)[1::2], Fetch((), [0]), 16)
    hid_b = finish(m_a, m, h.behind[half])
    sum_b = Sum(run, h, hid_b, blocks, mixed_b)
    sum_b.hop()
    for _ in range(1, half):
        sum_a.hop()
        sum_b.hop()
    out_a = sum_a.finish()
    out_b = sum_b.finish()

    top = out_a.reshape(n, rows, cols)
    low = out_b[: n * rows].reshape(n, rows, cols)
    tail = out_b[n * rows : n * rows + n].reshape(n, 1, cols)
    return jnp.concatenate([top, low, tail], axis=1).reshape(n * (local + 1), cols)


def solution(mesh):
    in_specs = (
        P(("grp", "tok"), None),
        P(("grp", "tok"), None),
        P("grp", None),
        P(("grp", "tok"), None),
        P(("grp", "tok"), None, None),
        P(("grp", "tok")),
        P(),
        P("grp", "tok"),
        P(None, "tok"),
        P("grp", None),
        P(),
        P(None, "tok"),
        P(None, "tok"),
        P("tok", None),
    )
    out_specs = P("grp", "tok")
    return jax.shard_map(shards, mesh=mesh, in_specs=in_specs, out_specs=out_specs, check_vma=False)
```

```python
import functools
import math

import jax
import jax.numpy as jnp
from jax import lax
from jax.experimental import pallas as pl
from jax.experimental.pallas import tpu as pltpu
from jax.sharding import PartitionSpec as P

D = 4096
H = 32
KVH = 8
HD = 128
GROUP = H // KVH
WIDTH = KVH * HD
EPS = 1e-05
NEG = -1e30
Z_CHIPS = 4

HBM = pl.BlockSpec(memory_space=pltpu.HBM)
VMEM = pl.BlockSpec(memory_space=pltpu.VMEM)
SMEM = pl.BlockSpec(memory_space=pltpu.SMEM)
F32 = jnp.float32
BF16 = jnp.bfloat16


def ring_order(n):
    columns = n // Z_CHIPS
    if n % Z_CHIPS or columns % 2:
        return list(range(n))
    order = [z * columns for z in range(Z_CHIPS)]
    for i, z in enumerate(reversed(range(Z_CHIPS))):
        xs = range(1, columns) if i % 2 == 0 else range(columns - 1, 0, -1)
        order += [z * columns + x for x in xs]
    return order


def params(mib):
    return pltpu.CompilerParams(vmem_limit_bytes=mib * 2**20)


STEP = pl.CostEstimate(flops=500_000_000, bytes_accessed=1_000_000, transcendentals=0)


def copies(pairs, sems):
    out = [pltpu.make_async_copy(src, dst, sems.at[i]) for i, (src, dst) in enumerate(pairs)]
    for c in out:
        c.start()
    return out


def in_hbm(x):
    return pltpu.with_memory_space_constraint(x, pltpu.HBM)


def pack_kernel(kv_ref, ask_ref, keys_ref, values_ref):
    rows = kv_ref.shape[0]
    for i in range(KVH):
        keys_ref[i * rows : (i + 1) * rows, :] = kv_ref[:, i * HD : (i + 1) * HD]
        values_ref[i * rows : (i + 1) * rows, :] = kv_ref[:, WIDTH + i * HD : WIDTH + (i + 1) * HD]
    ask = ask_ref[...].astype(F32)
    heads = jnp.concatenate([ask[:, i * HD : (i + 1) * HD] for i in range(H)], axis=0)
    keys_ref[KVH * rows :, :] = heads.astype(BF16)


def pack(kv, ask):
    rows = kv.shape[0]
    return pl.pallas_call(
        pack_kernel,
        out_shape=[
            pltpu.VMEM((KVH * rows + H, HD), BF16),
            pltpu.VMEM((KVH * rows, HD), BF16),
        ],
        in_specs=[VMEM, VMEM],
        out_specs=[VMEM, VMEM],
        cost_estimate=STEP,
        name="pack_keys",
    )(kv, ask)


def attention_kernel(count, first, rows, owners, q_in, seg_ref, *rest):
    parts, (out_ref, kv, q, sems) = rest[:count], rest[-4:]
    total = kv.shape[1]
    local = q_in.shape[0]
    moving = copies([(q_in.at[pl.ds(first, rows)], q)], sems)
    for j, part in enumerate(parts):
        at = pl.ds(pl.multiple_of(owners[j % (count // 2)] * local, 16), local)
        for i in range(KVH):
            kv[j // (count // 2) * KVH + i, at, :] = part[i * local : (i + 1) * local, :]
    key_pos = lax.broadcasted_iota(jnp.int32, (rows, total), 1)
    query_pos = lax.broadcasted_iota(jnp.int32, (rows, total), 0) + (owners[0] * local + first)
    span = jnp.broadcast_to(seg_ref[...], (rows, total)).astype(F32)
    own_span = jnp.sum(jnp.where(key_pos == query_pos, span, 0.0), axis=-1, keepdims=True)
    seen = (key_pos <= query_pos) & (span == own_span)
    bias = jnp.where(seen, 0.0, NEG).astype(F32)
    bias = jnp.concatenate([bias] * GROUP, axis=0)
    if len(rest) > count + 4:
        out_ref[H * rows :, :] = rest[count][...]
    moving[0].wait()
    for k in range(KVH):
        heads = range(k * GROUP, (k + 1) * GROUP)
        four = jnp.concatenate([q[:, i * HD : (i + 1) * HD] for i in heads], axis=0)
        s = lax.dot_general(four, kv[k], (((1,), (1,)), ((), ())), preferred_element_type=F32)
        s = s * (1.0 / math.sqrt(HD)) + bias
        w = jnp.exp(s - jnp.max(s, axis=-1, keepdims=True)).astype(BF16)
        t = jnp.sum(w.astype(F32), axis=-1, keepdims=True)
        o = jnp.dot(w, kv[KVH + k], preferred_element_type=F32) / t
        out_ref[k * GROUP * rows : (k + 1) * GROUP * rows, :] = o.astype(BF16)


def attention(first, rows, owners, q, seg, parts, dec=()):
    total = seg.shape[1]
    return pl.pallas_call(
        functools.partial(attention_kernel, len(parts), first, rows),
        out_shape=jax.ShapeDtypeStruct((H * (rows + len(dec)), HD), BF16),
        in_specs=[SMEM, HBM, VMEM] + [VMEM] * (len(parts) + len(dec)),
        out_specs=VMEM,
        scratch_shapes=[
            pltpu.VMEM((2 * KVH, total, HD), BF16),
            pltpu.VMEM((rows, D), BF16),
            pltpu.SemaphoreType.DMA((1,)),
        ],
        compiler_params=params(16),
        cost_estimate=STEP,
        name="prefill_attention",
    )(owners, q, seg, *parts, *dec)


def pick_kernel(n, groups, owners, slots, *rest):
    parts, outs = rest[:n], rest[n:]
    tok, grp = owners[0], owners[n]
    for j in range(groups):
        request = slots[(grp ^ j) * n + tok]
        for d, part in enumerate(parts):

            @pl.when(owners[d] == request % n)
            def _(part=part, out=outs[j]):
                out[...] = part[part.shape[0] - H :, :]


def pick(n, groups, owners, slots, parts):
    return pl.pallas_call(
        functools.partial(pick_kernel, n, groups),
        out_shape=[jax.ShapeDtypeStruct((H, HD), BF16) for _ in range(groups)],
        in_specs=[SMEM, SMEM] + [VMEM] * n,
        out_specs=[VMEM] * groups,
        compiler_params=params(16),
        cost_estimate=STEP,
        name="pick_queries",
    )(owners, slots, *parts)


def decode_kernel(n, groups, owners, slots, length, cache_in, *rest):
    choices, (out_ref, cache_ref, sems) = rest[:groups], rest[groups:]
    positions = cache_ref.shape[1]
    moving = copies([(cache_in, cache_ref)], sems)
    tok, grp = owners[0], owners[n]
    source = (slots[grp * n + tok] // n) ^ grp
    q = choices[0][...]
    for j in range(1, groups):
        q = jnp.where(source == j, choices[j][...], q)
    head = lax.broadcasted_iota(jnp.int32, (H, positions), 0) // GROUP
    moving[0].wait()
    s = jnp.zeros((H, positions), F32)
    for k in range(KVH):
        one = lax.dot_general(
            q, cache_ref[0, :, k * HD : (k + 1) * HD], (((1,), (1,)), ((), ())), preferred_element_type=F32
        )
        s = jnp.where(head == k, one, s)
    spot = lax.broadcasted_iota(jnp.int32, (H, positions), 1)
    s = jnp.where(spot < length[0], s * (1.0 / math.sqrt(HD)), NEG)
    w = jnp.exp(s - jnp.max(s, axis=-1, keepdims=True)).astype(BF16).astype(F32)
    t = jnp.sum(w, axis=-1, keepdims=True)
    o = jnp.zeros((H, HD), F32)
    for k in range(KVH):
        mine = jnp.where(head == k, w, 0.0).astype(BF16)
        o = o + jnp.dot(
            mine, cache_ref[0, :, WIDTH + k * HD : WIDTH + (k + 1) * HD], preferred_element_type=F32
        )
    out_ref[...] = (o / t).astype(BF16)


def decode(n, owners, slots, length, choices, cache):
    groups = len(choices)
    return pl.pallas_call(
        functools.partial(decode_kernel, n, groups),
        out_shape=jax.ShapeDtypeStruct((H, HD), BF16),
        in_specs=[SMEM, SMEM, SMEM, HBM] + [VMEM] * groups,
        out_specs=VMEM,
        scratch_shapes=[pltpu.VMEM(cache.shape, BF16), pltpu.SemaphoreType.DMA((1,))],
        compiler_params=params(16),
        cost_estimate=STEP,
        name="decode_attention",
    )(owners, slots, length, cache, *choices)


class Fetch:
    def __init__(self, gate=(), up=(), blocks=()):
        self.gate, self.up, self.blocks = tuple(gate), tuple(up), tuple(blocks)

    def shapes(self, cols, wide):
        out = [pltpu.VMEM((len(s) * cols, wide), BF16) for s in (self.gate, self.up) if s]
        return out + [pltpu.VMEM((wide, cols), BF16) for _ in self.blocks]

    def count(self):
        return len(self.gate) + len(self.up) + len(self.blocks)

    def outs(self):
        return (len(self.gate) > 0) + (len(self.up) > 0) + len(self.blocks)

    def keep(self, outs, store):
        outs = list(outs)
        if self.gate:
            store["gate", self.gate] = outs.pop(0)
        if self.up:
            store["up", self.up] = outs.pop(0)
        for block in self.blocks:
            store["down", block] = outs.pop(0)

    def start(self, owners, weights, outs, sems):
        pairs, outs = [], list(outs)
        for ref, shares in ((weights[0], self.gate), (weights[1], self.up)):
            if shares:
                out = outs.pop(0)
                cols = out.shape[0] // len(shares)
                for i, share in enumerate(shares):
                    at = pl.ds(pl.multiple_of(owners[share] * cols, cols), cols)
                    pairs.append((ref.at[at], out.at[pl.ds(i * cols, cols)]))
        for block in self.blocks:
            out = outs.pop(0)
            cols = out.shape[1]
            at = pl.ds(pl.multiple_of(owners[block] * cols, HD), cols)
            pairs.append((weights[2].at[:, at], out))
        return copies(pairs, sems)


def fetch_kernel(fetch, owners, *rest):
    for c in fetch.start(owners, rest[:3], rest[3:-1], rest[-1]):
        c.wait()


def fetch_early(fetch, owners, weights, cols, wide):
    shapes = fetch.shapes(cols, wide)
    return pl.pallas_call(
        functools.partial(fetch_kernel, fetch),
        out_shape=shapes,
        in_specs=[SMEM] + [HBM] * 3,
        out_specs=[VMEM] * len(shapes),
        scratch_shapes=[pltpu.SemaphoreType.DMA((fetch.count(),))],
        compiler_params=params(16),
        cost_estimate=STEP,
        name="fetch_weights",
    )(owners, *[in_hbm(x) for x in weights])


def project_kernel(n, rows, first, owners, *rest):
    parts, (wo_ref, resid_ref, out_ref, x, dec, resid) = rest[:n], rest[n:]
    resid[...] = resid_ref[...].astype(F32)
    local = resid.shape[0] // n
    wide = [resid[b * local + first : b * local + first + rows, :] for b in range(n)]
    for d, part in enumerate(parts):
        at = pl.ds(pl.multiple_of(owners[d] * rows, 16), rows)
        for i in range(H):
            x[at, i * HD : (i + 1) * HD] = part[i * rows : (i + 1) * rows, :]
        if part.shape[0] > H * rows:
            dec[pl.ds(pl.multiple_of(owners[d] * H, H), H), :] = part[H * rows :, :]
    spare = x.shape[0] - n * rows
    if spare:
        at = lax.broadcasted_iota(jnp.int32, (H * spare, n * H), 0)
        of = lax.broadcasted_iota(jnp.int32, (H * spare, n * H), 1)
        chosen = jnp.where(of == (at % spare) * H + at // spare, 1.0, 0.0).astype(BF16)
        heads = jnp.dot(chosen, dec[...], preferred_element_type=F32).astype(BF16)
        for i in range(H):
            x[n * rows :, i * HD : (i + 1) * HD] = heads[i * spare : (i + 1) * spare]
        wide += [resid[(b + 1) * local - 1 : (b + 1) * local, :] for b in range(n)]
        if spare > n:
            wide.append(jnp.zeros((spare - n, resid.shape[1]), F32))
    total = jnp.dot(x[...], wo_ref[...], preferred_element_type=F32)
    out_ref[...] = (jnp.concatenate(wide, axis=0) + total).astype(BF16)


def project(rows, spare, first, owners, parts, wo, resid):
    n = len(parts)
    m, cols = n * rows + spare, wo.shape[1]
    return pl.pallas_call(
        functools.partial(project_kernel, n, rows, first),
        out_shape=jax.ShapeDtypeStruct((m, cols), BF16),
        in_specs=[SMEM] + [VMEM] * (n + 2),
        out_specs=VMEM,
        scratch_shapes=[
            pltpu.VMEM((m, D), BF16),
            pltpu.VMEM((n * H, HD), BF16),
            pltpu.VMEM(resid.shape, F32),
        ],
        compiler_params=params(16),
        cost_estimate=STEP,
        name="out_projection",
    )(owners, *parts, wo, resid)


def scale_in(x, squares, tenants, gain_ref, at):
    for j in range(0, x.shape[1], HD):
        squares = squares + x[:, j : j + HD] * x[:, j : j + HD]
    gain = jnp.broadcast_to(gain_ref[0:1, at], x.shape)
    for t in range(1, gain_ref.shape[0]):
        gain = jnp.where(tenants == t, gain_ref[t : t + 1, at], gain)
    return squares, (x * gain).astype(BF16)


def feed_kernel(lo, hi, shares, taken, fetch, owners, tenants_ref, gain_ref, *rest):
    weights, rest = rest[:3], rest[3:]
    w_refs, rest = rest[:2], rest[2:]
    chunks = (len(rest) - 5 - fetch.outs() - 3 * taken) // len(shares)
    parts, rest = rest[: chunks * len(shares)], rest[chunks * len(shares) :]
    held, rest = (rest[:3], rest[3:]) if taken else (None, rest)
    (gates, lifts, squares), fetched, (scaled, sems) = rest[:3], rest[3:-2], rest[-2:]
    moving = fetch.start(owners, weights, fetched, sems)
    cols = parts[0].shape[1]
    tenants = tenants_ref[lo:hi, :]
    total = held[2][lo:hi, :] if taken else jnp.zeros((hi - lo, HD), F32)
    for i, share in enumerate(shares):
        x = jnp.concatenate([p[...] for p in parts[chunks * i : chunks * (i + 1)]], axis=0).astype(F32)
        at = pl.ds(pl.multiple_of(owners[share] * cols, HD), cols)
        total, x = scale_in(x, total, tenants, gain_ref, at)
        scaled[:, i * cols : (i + 1) * cols] = x
    squares[lo:hi, :] = total
    for i, out in enumerate((gates, lifts)):
        one = jnp.dot(scaled[...], w_refs[i][...], preferred_element_type=F32)
        out[lo:hi, :] = held[i][lo:hi, :] + one if taken else one
    for c in moving:
        c.wait()


def feed(lo, hi, shares, owners, tenants, gain, weights, w, parts, held, fetch):
    m, wide = tenants.shape[0], w[0].shape[1]
    cols = parts[0].shape[1]
    first = 6 + len(w) + len(parts)
    fetched = fetch.shapes(cols, wide)
    sums = [jax.ShapeDtypeStruct((m, wide), F32)] * 2 + [jax.ShapeDtypeStruct((m, HD), F32)]
    return pl.pallas_call(
        functools.partial(feed_kernel, lo, hi, shares, len(held) > 0, fetch),
        out_shape=sums + fetched,
        in_specs=[SMEM, VMEM, VMEM] + [HBM] * 3 + [VMEM] * (len(w) + len(parts) + len(held)),
        out_specs=[VMEM] * (3 + len(fetched)),
        scratch_shapes=[
            pltpu.VMEM((hi - lo, cols * len(shares)), BF16),
            pltpu.SemaphoreType.DMA((max(fetch.count(), 1),)),
        ],
        input_output_aliases={first + i: i for i in range(len(held))},
        compiler_params=params(16),
        cost_estimate=STEP,
        name="gate_up_sum",
    )(owners, tenants, gain, *[in_hbm(x) for x in weights], *w, *parts, *held)


def hidden_kernel(lo, hi, share, owners, tenants_ref, gain_ref, w_gate, w_up, part, gates, lifts, squares, out):
    cols = part.shape[1]
    at = pl.ds(pl.multiple_of(owners[share] * cols, HD), cols)
    total, x = scale_in(part[...].astype(F32), squares[lo:hi, :], tenants_ref[lo:hi, :], gain_ref, at)
    scale = lax.rsqrt(jnp.sum(total, axis=-1, keepdims=True) / D + EPS)
    gate = (gates[lo:hi, :] + jnp.dot(x, w_gate[...], preferred_element_type=F32)) * scale
    gate = gate / (1.0 + jnp.exp(-gate))
    lift = (lifts[lo:hi, :] + jnp.dot(x, w_up[...], preferred_element_type=F32)) * scale
    out[...] = (gate * lift).astype(BF16)


def hide(lo, hi, share, owners, tenants, gain, w, part, held):
    return pl.pallas_call(
        functools.partial(hidden_kernel, lo, hi, share),
        out_shape=jax.ShapeDtypeStruct((hi - lo, w[0].shape[1]), BF16),
        in_specs=[SMEM] + [VMEM] * 8,
        out_specs=VMEM,
        compiler_params=params(16),
        cost_estimate=STEP,
        name="hidden",
    )(owners, tenants, gain, *w, part, *held)


def assemble_kernel(n, rows, owners, hidden, w, fw, bw, own, top, out, block):
    total = jnp.dot(hidden[...], w[...], preferred_element_type=F32)
    total = total + fw[...].astype(F32) + bw[...].astype(F32) + own[...].astype(F32)
    local = block.shape[0] // n
    for b in range(n):
        at = b * local
        block[at : at + rows, :] = top[b * rows : (b + 1) * rows, :].astype(F32)
        block[at + rows : at + 2 * rows, :] = total[b * rows : (b + 1) * rows, :]
        block[at + 2 * rows : at + local, :] = total[n * rows + b : n * rows + b + 1, :]
    out[...] = block[...].astype(BF16)


def assemble(n, rows, owners, hidden, w, arrived, own, top):
    shape = (n * (2 * rows + 1), top.shape[1])
    return pl.pallas_call(
        functools.partial(assemble_kernel, n, rows),
        out_shape=jax.ShapeDtypeStruct(shape, BF16),
        in_specs=[SMEM] + [VMEM] * 6,
        out_specs=VMEM,
        scratch_shapes=[pltpu.VMEM(shape, F32)],
        compiler_params=params(16),
        cost_estimate=STEP,
        name="last_sum",
    )(owners, hidden, w, *arrived, own, top)


def down_kernel(flags, own, owners, hidden, *rest):
    count = len(flags)
    weights, rest = rest[:count], rest[count:]
    terms, outs = rest[: sum(flags) + own], rest[sum(flags) + own :]
    taken = 0
    for i in range(count):
        total = jnp.dot(hidden[...], weights[i][...], preferred_element_type=F32)
        for term in terms[taken : taken + flags[i] + own]:
            total = total + term[...].astype(F32)
        taken += flags[i]
        outs[i][...] = total.astype(BF16)


def down(flags, owners, hidden, weights, arrived, own=()):
    m, cols = hidden.shape[0], weights[0].shape[1]
    return pl.pallas_call(
        functools.partial(down_kernel, flags, len(own)),
        out_shape=[jax.ShapeDtypeStruct((m, cols), BF16) for _ in flags],
        in_specs=[SMEM] + [VMEM] * (1 + len(flags) + len(arrived) + len(own)),
        out_specs=[VMEM] * len(flags),
        compiler_params=params(16),
        cost_estimate=STEP,
        name="down_sum",
    )(owners, hidden, *weights, *arrived, *own)


class Chain:
    def __init__(self, n, order, own, last):
        self.n, self.half, self.last = n, n // 2, last
        self.fw = [(order[i], order[(i + 1) % n]) for i in range(n)]
        self.bw = [(b, a) for a, b in self.fw]
        self.own, self.ahead, self.behind, self.hops = own, [own], [own], 0

    def done(self):
        return self.hops == self.half

    def parts(self):
        return [self.own] + self.ahead[1:] + self.behind[:0:-1]


def settle_kernel(*refs):
    for i in range(len(refs) // 2):
        refs[len(refs) // 2 + i][...] = refs[i][...]


def settle(*arrays):
    return pl.pallas_call(
        settle_kernel,
        out_shape=[jax.ShapeDtypeStruct(x.shape, x.dtype) for x in arrays],
        in_specs=[VMEM] * len(arrays),
        out_specs=[VMEM] * len(arrays),
        cost_estimate=STEP,
        name="settle",
    )(*arrays)


def tick_kernel(token, out):
    out[...] = token[...]


def tick(token):
    return pl.pallas_call(
        tick_kernel,
        out_shape=jax.ShapeDtypeStruct(token.shape, token.dtype),
        in_specs=[VMEM],
        out_specs=VMEM,
        cost_estimate=STEP,
        name="tick",
    )(token)


class Order:
    def __init__(self, ids):
        self.ids, self.last = ids, ()
        self.token = jnp.zeros((8, HD), F32)

    def after(self):
        return lax.optimization_barrier((self.ids, *self.last))[0]

    def mark(self, *out):
        self.last = out
        return out[0]

    def tick(self):
        self.token = tick(lax.optimization_barrier((self.token, *self.last))[0])

    def tied(self, *arrays):
        out = lax.optimization_barrier((*arrays, self.token, *self.last))
        self.last, self.token = (out[0],), out[len(arrays)]
        return out[: len(arrays)]

    def hop(self, chain):
        chain.hops += 1
        f, b = chain.ahead[-1], chain.behind[-1]
        f, b = self.tied(f, b)
        if chain.done() and chain.last == "fw":
            chain.ahead.append(lax.ppermute(f, "tok", chain.fw))
        elif chain.done():
            chain.behind.append(lax.ppermute(b, "tok", chain.bw))
        else:
            chain.ahead.append(lax.ppermute(f, "tok", chain.fw))
            chain.behind.append(lax.ppermute(b, "tok", chain.bw))


class Sum:
    def __init__(self, run, chain, hidden, blocks, own):
        self.run, self.chain, self.hidden, self.blocks = run, chain, hidden, blocks
        self.own, self.step, self.arrived = own, 0, ()

    def call(self, blocks, flags, own=()):
        weights = [self.blocks["down", -b % self.chain.n] for b in blocks]
        out = down(flags, self.run.after(), self.hidden, weights, self.arrived, own)
        self.run.mark(out[0])
        return out

    def hop(self):
        chain = self.chain
        d, forward = chain.half - self.step, chain.last == "fw"
        if self.step == 0:
            out = self.run.tied(*self.call([d], [0]))
            self.arrived = (lax.ppermute(out[0], "tok", chain.fw if forward else chain.bw),)
        else:
            flags = [1, 1] if self.step > 1 else ([1, 0] if forward else [0, 1])
            out = self.run.tied(*self.call([d, -d], flags))
            self.arrived = (lax.ppermute(out[0], "tok", chain.fw), lax.ppermute(out[1], "tok", chain.bw))
        self.step += 1

    def finish(self):
        return self.call([0], [2], (self.own,))[0]


def shards(
    pre_q,
    pre_kv,
    pre_segment,
    dec_q,
    cache,
    cache_len,
    slot_request,
    resid,
    wo,
    tenant,
    norm_gain,
    w_gate,
    w_up,
    w_down,
):
    n, groups = lax.axis_size("tok"), lax.axis_size("grp")
    tok, grp = lax.axis_index("tok"), lax.axis_index("grp")
    local = pre_q.shape[0]
    rows = local // 2
    cols = wo.shape[1]
    half = n // 2
    spare = -(-n // 16) * 16
    order = ring_order(n)
    ids = jnp.arange(n, dtype=jnp.int32)
    place = sum(jnp.where(tok == t, i, 0) for i, t in enumerate(order)).astype(jnp.int32)
    spots = (place - ids) % n
    owners = sum(jnp.where(spots == i, t, 0) for i, t in enumerate(order)).astype(jnp.int32)
    owners = jnp.concatenate([owners, jnp.reshape(grp, (1,)).astype(jnp.int32)])

    def split(a):
        a = a.reshape(n, local + 1, -1)
        first = a[:, :rows].reshape(n * rows, -1)
        second = a[:, rows:local].reshape(n * rows, -1)
        tail = jnp.pad(a[:, local], ((0, spare - n), (0, 0)))
        return first, jnp.concatenate([second, tail], axis=0)

    tenants = jnp.concatenate(split(tenant[0][:, None]), axis=0)
    run = Order(owners)

    def chain(own, last):
        return Chain(n, order, own, last)

    own_keys, own_values = pack(pre_kv, dec_q)
    keys, values = chain(own_keys, "fw"), chain(own_values, "bw")
    run.hop(keys)
    run.tick()
    run.hop(values)
    tenants, gain = settle(tenants, norm_gain)
    run.mark(*run.last, tenants, owners)
    while not keys.done():
        run.tick()
        run.hop(keys)
        run.tick()
        run.hop(values)
    choices = list(pick(n, groups, run.after(), slot_request, keys.parts()))
    run.mark(choices[0])
    for j in range(1, groups):
        (choices[j],) = run.tied(choices[j])
        choices[j] = lax.ppermute(choices[j], "grp", [(i, i ^ j) for i in range(groups)])
    kv = keys.parts() + values.parts()
    a = chain(run.mark(attention(0, rows, run.after(), pre_q, pre_segment, kv)), "fw")
    run.hop(a)
    dec = run.mark(decode(n, run.after(), slot_request, cache_len, choices, cache))
    b = chain(run.mark(attention(rows, rows, run.after(), pre_q, pre_segment, kv, (dec,))), "bw")
    run.hop(b)
    run.hop(a)
    weights = (w_gate, w_up, w_down)
    wide = w_gate.shape[1]
    far = [d for d in range(half - 1, half + 2)]
    fetches = [
        Fetch([0], [0]),
        Fetch([1, n - 1]),
        Fetch((), [1, n - 1]),
        Fetch([half], [half]),
    ]
    fetches.insert(0, Fetch((), (), far))
    store = {}

    def fetch_some():
        if fetches:
            fetch = fetches.pop(0)
            out = fetch_early(fetch, run.after(), weights, cols, wide)
            run.mark(out[0])
            fetch.keep(out, store)

    fetch_some()
    run.hop(b)
    fetch_some()
    while not a.done():
        run.hop(a)
        fetch_some()
        run.hop(b)
        fetch_some()
    while fetches:
        fetch_some()
    mixed_a = run.mark(project(rows, 0, 0, run.after(), a.parts(), wo, resid))
    g = chain(mixed_a, "fw")
    run.hop(g)
    mixed_b = run.mark(project(rows, spare, rows, run.after(), b.parts(), wo, resid))
    h = chain(mixed_b, "bw")
    run.hop(h)

    m_a, m = mixed_a.shape[0], tenants.shape[0]
    held = ()

    def add(lo, hi, shares, parts, fetch):
        w = [store["gate", tuple(shares)], store["up", tuple(shares)]]
        out = feed(lo, hi, shares, run.after(), tenants, gain, weights, w, parts, held, fetch)
        run.mark(out[2])
        fetch.keep(out[3:], store)
        return out[:3]

    def arrived(i):
        return [g.ahead[i], h.ahead[i], g.behind[i], h.behind[i]]

    def pair(i):
        return [i, n - i] if 1 < i < half else []

    def missing(ds):
        return [d for d in ds if ("down", d) not in store]

    held = add(0, m, [0], [mixed_a, mixed_b], Fetch(pair(2)))
    run.hop(g)
    run.hop(h)
    for i in range(1, half - 1):
        more = missing([half - 2, half + 2]) if i == half - 2 else []
        held = add(0, m, [i, n - i], arrived(i), Fetch(pair(i + 2), pair(i + 1), more))
        run.hop(g)
        run.hop(h)
    i = half - 1
    held = add(0, m_a, [i, n - i], arrived(i)[::2], Fetch((), (), missing(range(1, n))))

    last = [store["gate", (half,)], store["up", (half,)]]

    def finish(lo, hi, part):
        return run.mark(hide(lo, hi, half, run.after(), tenants, gain, last, part, held))

    hid_a = finish(0, m_a, g.ahead[half])
    sum_a = Sum(run, g, hid_a, store, mixed_a)
    sum_a.hop()
    held = add(m_a, m, [i, n - i], arrived(i)[1::2], Fetch((), (), [0]))
    hid_b = finish(m_a, m, h.behind[half])
    sum_b = Sum(run, h, hid_b, store, mixed_b)
    sum_b.hop()
    for _ in range(1, half):
        sum_a.hop()
        sum_b.hop()
    out_a = sum_a.finish()
    return assemble(n, rows, run.after(), hid_b, store["down", 0], sum_b.arrived, mixed_b, out_a)


def solution(mesh):
    in_specs = (
        P(("grp", "tok"), None),
        P(("grp", "tok"), None),
        P("grp", None),
        P(("grp", "tok"), None),
        P(("grp", "tok"), None, None),
        P(("grp", "tok")),
        P(),
        P("grp", "tok"),
        P(None, "tok"),
        P("grp", None),
        P(),
        P(None, "tok"),
        P(None, "tok"),
        P("tok", None),
    )
    out_specs = P("grp", "tok")
    return jax.shard_map(shards, mesh=mesh, in_specs=in_specs, out_specs=out_specs, check_vma=False)
```

```python
import functools
import math

import jax
import jax.numpy as jnp
from jax import lax
from jax.experimental import pallas as pl
from jax.experimental.pallas import tpu as pltpu
from jax.sharding import PartitionSpec as P

D = 4096
H = 32
KVH = 8
HD = 128
GROUP = H // KVH
WIDTH = KVH * HD
EPS = 1e-05
NEG = -1e30
Z_CHIPS = 4

HBM = pl.BlockSpec(memory_space=pltpu.HBM)
VMEM = pl.BlockSpec(memory_space=pltpu.VMEM)
SMEM = pl.BlockSpec(memory_space=pltpu.SMEM)
F32 = jnp.float32
BF16 = jnp.bfloat16


def ring_order(n):
    columns = n // Z_CHIPS
    if n % Z_CHIPS or columns % 2:
        return list(range(n))
    order = [z * columns for z in range(Z_CHIPS)]
    for i, z in enumerate(reversed(range(Z_CHIPS))):
        xs = range(1, columns) if i % 2 == 0 else range(columns - 1, 0, -1)
        order += [z * columns + x for x in xs]
    return order


def params(mib):
    return pltpu.CompilerParams(vmem_limit_bytes=mib * 2**20)


STEP = pl.CostEstimate(flops=500_000_000, bytes_accessed=1_000_000, transcendentals=0)


def copies(pairs, sems):
    out = [pltpu.make_async_copy(src, dst, sems.at[i]) for i, (src, dst) in enumerate(pairs)]
    for c in out:
        c.start()
    return out


def in_hbm(x):
    return pltpu.with_memory_space_constraint(x, pltpu.HBM)


def pack_kernel(kv_ref, ask_ref, keys_ref, values_ref):
    rows = kv_ref.shape[0]
    for i in range(KVH):
        keys_ref[i * rows : (i + 1) * rows, :] = kv_ref[:, i * HD : (i + 1) * HD]
        values_ref[i * rows : (i + 1) * rows, :] = kv_ref[:, WIDTH + i * HD : WIDTH + (i + 1) * HD]
    ask = ask_ref[...].astype(F32)
    heads = jnp.concatenate([ask[:, i * HD : (i + 1) * HD] for i in range(H)], axis=0)
    keys_ref[KVH * rows :, :] = heads.astype(BF16)


def pack(kv, ask):
    rows = kv.shape[0]
    return pl.pallas_call(
        pack_kernel,
        out_shape=[
            pltpu.VMEM((KVH * rows + H, HD), BF16),
            pltpu.VMEM((KVH * rows, HD), BF16),
        ],
        in_specs=[VMEM, VMEM],
        out_specs=[VMEM, VMEM],
        cost_estimate=STEP,
        name="pack_keys",
    )(kv, ask)


def attention_kernel(count, first, rows, owners, q_in, seg_ref, *rest):
    parts, (out_ref, kv, q, sems) = rest[:count], rest[-4:]
    total = kv.shape[1]
    local = q_in.shape[0]
    moving = copies([(q_in.at[pl.ds(first, rows)], q)], sems)
    for j, part in enumerate(parts):
        at = pl.ds(pl.multiple_of(owners[j % (count // 2)] * local, 16), local)
        for i in range(KVH):
            kv[j // (count // 2) * KVH + i, at, :] = part[i * local : (i + 1) * local, :]
    key_pos = lax.broadcasted_iota(jnp.int32, (rows, total), 1)
    query_pos = lax.broadcasted_iota(jnp.int32, (rows, total), 0) + (owners[0] * local + first)
    span = jnp.broadcast_to(seg_ref[...], (rows, total)).astype(F32)
    own_span = jnp.sum(jnp.where(key_pos == query_pos, span, 0.0), axis=-1, keepdims=True)
    seen = (key_pos <= query_pos) & (span == own_span)
    bias = jnp.where(seen, 0.0, NEG).astype(F32)
    bias = jnp.concatenate([bias] * GROUP, axis=0)
    if len(rest) > count + 4:
        out_ref[H * rows :, :] = rest[count][...]
    moving[0].wait()
    for k in range(KVH):
        heads = range(k * GROUP, (k + 1) * GROUP)
        four = jnp.concatenate([q[:, i * HD : (i + 1) * HD] for i in heads], axis=0)
        s = lax.dot_general(four, kv[k], (((1,), (1,)), ((), ())), preferred_element_type=F32)
        s = s * (1.0 / math.sqrt(HD)) + bias
        w = jnp.exp(s - jnp.max(s, axis=-1, keepdims=True)).astype(BF16)
        t = jnp.sum(w.astype(F32), axis=-1, keepdims=True)
        o = jnp.dot(w, kv[KVH + k], preferred_element_type=F32) / t
        out_ref[k * GROUP * rows : (k + 1) * GROUP * rows, :] = o.astype(BF16)


def attention(first, rows, owners, q, seg, parts, dec=()):
    total = seg.shape[1]
    return pl.pallas_call(
        functools.partial(attention_kernel, len(parts), first, rows),
        out_shape=jax.ShapeDtypeStruct((H * (rows + len(dec)), HD), BF16),
        in_specs=[SMEM, HBM, VMEM] + [VMEM] * (len(parts) + len(dec)),
        out_specs=VMEM,
        scratch_shapes=[
            pltpu.VMEM((2 * KVH, total, HD), BF16),
            pltpu.VMEM((rows, D), BF16),
            pltpu.SemaphoreType.DMA((1,)),
        ],
        compiler_params=params(16),
        cost_estimate=STEP,
        name="prefill_attention",
    )(owners, q, seg, *parts, *dec)


def pick_kernel(n, groups, owners, slots, *rest):
    parts, outs = rest[:n], rest[n:]
    tok, grp = owners[0], owners[n]
    for j in range(groups):
        request = slots[(grp ^ j) * n + tok]
        for d, part in enumerate(parts):

            @pl.when(owners[d] == request % n)
            def _(part=part, out=outs[j]):
                out[...] = part[part.shape[0] - H :, :]


def pick(n, groups, owners, slots, parts):
    return pl.pallas_call(
        functools.partial(pick_kernel, n, groups),
        out_shape=[jax.ShapeDtypeStruct((H, HD), BF16) for _ in range(groups)],
        in_specs=[SMEM, SMEM] + [VMEM] * n,
        out_specs=[VMEM] * groups,
        compiler_params=params(16),
        cost_estimate=STEP,
        name="pick_queries",
    )(owners, slots, *parts)


def decode_kernel(n, groups, owners, slots, length, cache_in, *rest):
    choices, (out_ref, cache_ref, sems) = rest[:groups], rest[groups:]
    positions = cache_ref.shape[1]
    moving = copies([(cache_in, cache_ref)], sems)
    tok, grp = owners[0], owners[n]
    source = (slots[grp * n + tok] // n) ^ grp
    q = choices[0][...]
    for j in range(1, groups):
        q = jnp.where(source == j, choices[j][...], q)
    head = lax.broadcasted_iota(jnp.int32, (H, positions), 0) // GROUP
    moving[0].wait()
    s = jnp.zeros((H, positions), F32)
    for k in range(KVH):
        one = lax.dot_general(
            q, cache_ref[0, :, k * HD : (k + 1) * HD], (((1,), (1,)), ((), ())), preferred_element_type=F32
        )
        s = jnp.where(head == k, one, s)
    spot = lax.broadcasted_iota(jnp.int32, (H, positions), 1)
    s = jnp.where(spot < length[0], s * (1.0 / math.sqrt(HD)), NEG)
    w = jnp.exp(s - jnp.max(s, axis=-1, keepdims=True)).astype(BF16).astype(F32)
    t = jnp.sum(w, axis=-1, keepdims=True)
    o = jnp.zeros((H, HD), F32)
    for k in range(KVH):
        mine = jnp.where(head == k, w, 0.0).astype(BF16)
        o = o + jnp.dot(
            mine, cache_ref[0, :, WIDTH + k * HD : WIDTH + (k + 1) * HD], preferred_element_type=F32
        )
    out_ref[...] = (o / t).astype(BF16)


def decode(n, owners, slots, length, choices, cache):
    groups = len(choices)
    return pl.pallas_call(
        functools.partial(decode_kernel, n, groups),
        out_shape=jax.ShapeDtypeStruct((H, HD), BF16),
        in_specs=[SMEM, SMEM, SMEM, HBM] + [VMEM] * groups,
        out_specs=VMEM,
        scratch_shapes=[pltpu.VMEM(cache.shape, BF16), pltpu.SemaphoreType.DMA((1,))],
        compiler_params=params(16),
        cost_estimate=STEP,
        name="decode_attention",
    )(owners, slots, length, cache, *choices)


class Fetch:
    def __init__(self, gate=(), up=(), blocks=()):
        self.gate, self.up, self.blocks = tuple(gate), tuple(up), tuple(blocks)

    def shapes(self, cols, wide):
        out = [pltpu.VMEM((len(s) * cols, wide), BF16) for s in (self.gate, self.up) if s]
        return out + [pltpu.VMEM((wide, cols), BF16) for _ in self.blocks]

    def count(self):
        return len(self.gate) + len(self.up) + len(self.blocks)

    def outs(self):
        return (len(self.gate) > 0) + (len(self.up) > 0) + len(self.blocks)

    def keep(self, outs, store):
        outs = list(outs)
        if self.gate:
            store["gate", self.gate] = outs.pop(0)
        if self.up:
            store["up", self.up] = outs.pop(0)
        for block in self.blocks:
            store["down", block] = outs.pop(0)

    def start(self, owners, weights, outs, sems):
        pairs, outs = [], list(outs)
        for ref, shares in ((weights[0], self.gate), (weights[1], self.up)):
            if shares:
                out = outs.pop(0)
                cols = out.shape[0] // len(shares)
                for i, share in enumerate(shares):
                    at = pl.ds(pl.multiple_of(owners[share] * cols, cols), cols)
                    pairs.append((ref.at[at], out.at[pl.ds(i * cols, cols)]))
        for block in self.blocks:
            out = outs.pop(0)
            cols = out.shape[1]
            at = pl.ds(pl.multiple_of(owners[block] * cols, HD), cols)
            pairs.append((weights[2].at[:, at], out))
        return copies(pairs, sems)


def fetch_kernel(fetch, owners, *rest):
    for c in fetch.start(owners, rest[:3], rest[3:-1], rest[-1]):
        c.wait()


def fetch_early(fetch, owners, weights, cols, wide):
    shapes = fetch.shapes(cols, wide)
    return pl.pallas_call(
        functools.partial(fetch_kernel, fetch),
        out_shape=shapes,
        in_specs=[SMEM] + [HBM] * 3,
        out_specs=[VMEM] * len(shapes),
        scratch_shapes=[pltpu.SemaphoreType.DMA((fetch.count(),))],
        compiler_params=params(16),
        cost_estimate=STEP,
        name="fetch_weights",
    )(owners, *[in_hbm(x) for x in weights])


def project_kernel(n, rows, first, owners, *rest):
    parts, (wo_ref, resid_ref, out_ref, x, dec, resid) = rest[:n], rest[n:]
    resid[...] = resid_ref[...].astype(F32)
    local = resid.shape[0] // n
    wide = [resid[b * local + first : b * local + first + rows, :] for b in range(n)]
    for d, part in enumerate(parts):
        at = pl.ds(pl.multiple_of(owners[d] * rows, 16), rows)
        for i in range(H):
            x[at, i * HD : (i + 1) * HD] = part[i * rows : (i + 1) * rows, :]
        if part.shape[0] > H * rows:
            dec[pl.ds(pl.multiple_of(owners[d] * H, H), H), :] = part[H * rows :, :]
    spare = x.shape[0] - n * rows
    if spare:
        at = lax.broadcasted_iota(jnp.int32, (H * spare, n * H), 0)
        of = lax.broadcasted_iota(jnp.int32, (H * spare, n * H), 1)
        chosen = jnp.where(of == (at % spare) * H + at // spare, 1.0, 0.0).astype(BF16)
        heads = jnp.dot(chosen, dec[...], preferred_element_type=F32).astype(BF16)
        for i in range(H):
            x[n * rows :, i * HD : (i + 1) * HD] = heads[i * spare : (i + 1) * spare]
        wide += [resid[(b + 1) * local - 1 : (b + 1) * local, :] for b in range(n)]
        if spare > n:
            wide.append(jnp.zeros((spare - n, resid.shape[1]), F32))
    total = jnp.dot(x[...], wo_ref[...], preferred_element_type=F32)
    out_ref[...] = (jnp.concatenate(wide, axis=0) + total).astype(BF16)


def project(rows, spare, first, owners, parts, wo, resid):
    n = len(parts)
    m, cols = n * rows + spare, wo.shape[1]
    return pl.pallas_call(
        functools.partial(project_kernel, n, rows, first),
        out_shape=jax.ShapeDtypeStruct((m, cols), BF16),
        in_specs=[SMEM] + [VMEM] * (n + 2),
        out_specs=VMEM,
        scratch_shapes=[
            pltpu.VMEM((m, D), BF16),
            pltpu.VMEM((n * H, HD), BF16),
            pltpu.VMEM(resid.shape, F32),
        ],
        compiler_params=params(16),
        cost_estimate=STEP,
        name="out_projection",
    )(owners, *parts, wo, resid)


def scale_in(x, squares, tenants, gain_ref, at):
    for j in range(0, x.shape[1], HD):
        squares = squares + x[:, j : j + HD] * x[:, j : j + HD]
    gain = jnp.broadcast_to(gain_ref[0:1, at], x.shape)
    for t in range(1, gain_ref.shape[0]):
        gain = jnp.where(tenants == t, gain_ref[t : t + 1, at], gain)
    return squares, (x * gain).astype(BF16)


def feed_kernel(lo, hi, shares, taken, fetch, owners, tenants_ref, gain_ref, *rest):
    weights, rest = rest[:3], rest[3:]
    w_refs, rest = rest[:2], rest[2:]
    chunks = (len(rest) - 5 - fetch.outs() - 3 * taken) // len(shares)
    parts, rest = rest[: chunks * len(shares)], rest[chunks * len(shares) :]
    held, rest = (rest[:3], rest[3:]) if taken else (None, rest)
    (gates, lifts, squares), fetched, (scaled, sems) = rest[:3], rest[3:-2], rest[-2:]
    moving = fetch.start(owners, weights, fetched, sems)
    cols = parts[0].shape[1]
    tenants = tenants_ref[lo:hi, :]
    total = held[2][lo:hi, :] if taken else jnp.zeros((hi - lo, HD), F32)
    for i, share in enumerate(shares):
        x = jnp.concatenate([p[...] for p in parts[chunks * i : chunks * (i + 1)]], axis=0).astype(F32)
        at = pl.ds(pl.multiple_of(owners[share] * cols, HD), cols)
        total, x = scale_in(x, total, tenants, gain_ref, at)
        scaled[:, i * cols : (i + 1) * cols] = x
    squares[lo:hi, :] = total
    for i, out in enumerate((gates, lifts)):
        one = jnp.dot(scaled[...], w_refs[i][...], preferred_element_type=F32)
        out[lo:hi, :] = held[i][lo:hi, :] + one if taken else one
    for c in moving:
        c.wait()


def feed(lo, hi, shares, owners, tenants, gain, weights, w, parts, held, fetch):
    m, wide = tenants.shape[0], w[0].shape[1]
    cols = parts[0].shape[1]
    first = 6 + len(w) + len(parts)
    fetched = fetch.shapes(cols, wide)
    sums = [jax.ShapeDtypeStruct((m, wide), F32)] * 2 + [jax.ShapeDtypeStruct((m, HD), F32)]
    return pl.pallas_call(
        functools.partial(feed_kernel, lo, hi, shares, len(held) > 0, fetch),
        out_shape=sums + fetched,
        in_specs=[SMEM, VMEM, VMEM] + [HBM] * 3 + [VMEM] * (len(w) + len(parts) + len(held)),
        out_specs=[VMEM] * (3 + len(fetched)),
        scratch_shapes=[
            pltpu.VMEM((hi - lo, cols * len(shares)), BF16),
            pltpu.SemaphoreType.DMA((max(fetch.count(), 1),)),
        ],
        input_output_aliases={first + i: i for i in range(len(held))},
        compiler_params=params(16),
        cost_estimate=STEP,
        name="gate_up_sum",
    )(owners, tenants, gain, *[in_hbm(x) for x in weights], *w, *parts, *held)


def hidden_kernel(lo, hi, share, owners, tenants_ref, gain_ref, w_gate, w_up, part, gates, lifts, squares, out):
    cols = part.shape[1]
    at = pl.ds(pl.multiple_of(owners[share] * cols, HD), cols)
    total, x = scale_in(part[...].astype(F32), squares[lo:hi, :], tenants_ref[lo:hi, :], gain_ref, at)
    scale = lax.rsqrt(jnp.sum(total, axis=-1, keepdims=True) / D + EPS)
    gate = (gates[lo:hi, :] + jnp.dot(x, w_gate[...], preferred_element_type=F32)) * scale
    gate = gate / (1.0 + jnp.exp(-gate))
    lift = (lifts[lo:hi, :] + jnp.dot(x, w_up[...], preferred_element_type=F32)) * scale
    out[...] = (gate * lift).astype(BF16)


def hide(lo, hi, share, owners, tenants, gain, w, part, held):
    return pl.pallas_call(
        functools.partial(hidden_kernel, lo, hi, share),
        out_shape=jax.ShapeDtypeStruct((hi - lo, w[0].shape[1]), BF16),
        in_specs=[SMEM] + [VMEM] * 8,
        out_specs=VMEM,
        compiler_params=params(16),
        cost_estimate=STEP,
        name="hidden",
    )(owners, tenants, gain, *w, part, *held)


def last_block(hidden, w, fw, bw, own):
    total = jnp.dot(hidden[...], w[...], preferred_element_type=F32)
    return total + fw[...].astype(F32) + bw[...].astype(F32) + own[...].astype(F32)


def place_kernel(n, rows, owners, hidden, w, fw, bw, own, hidden_b, own_b, block, part):
    part[...] = jnp.dot(hidden_b[...], w[...], preferred_element_type=F32) + own_b[...].astype(F32)
    total = last_block(hidden, w, fw, bw, own)
    local = block.shape[0] // n
    for b in range(n):
        block[b * local : b * local + rows, :] = total[b * rows : (b + 1) * rows, :]


def put_rows(n, rows, owners, hidden, w, arrived, own, hidden_b, own_b):
    return pl.pallas_call(
        functools.partial(place_kernel, n, rows),
        out_shape=[pltpu.VMEM((n * (2 * rows + 1), own.shape[1]), F32), pltpu.VMEM(own_b.shape, F32)],
        in_specs=[SMEM] + [VMEM] * 7,
        out_specs=[VMEM, VMEM],
        compiler_params=params(16),
        cost_estimate=STEP,
        name="place_sum",
    )(owners, hidden, w, *arrived, own, hidden_b, own_b)


def assemble_kernel(n, rows, owners, fw, bw, part, placed, out, block):
    total = part[...] + fw[...].astype(F32) + bw[...].astype(F32)
    local = block.shape[0] // n
    for b in range(n):
        at = b * local + rows
        block[at : at + rows, :] = total[b * rows : (b + 1) * rows, :]
        block[at + rows : at + rows + 1, :] = total[n * rows + b : n * rows + b + 1, :]
    out[...] = block[...].astype(BF16)


def assemble(n, rows, owners, arrived, part, placed):
    return pl.pallas_call(
        functools.partial(assemble_kernel, n, rows),
        out_shape=[jax.ShapeDtypeStruct(placed.shape, BF16), pltpu.VMEM(placed.shape, F32)],
        in_specs=[SMEM] + [VMEM] * 4,
        out_specs=[VMEM, VMEM],
        input_output_aliases={4: 1},
        compiler_params=params(16),
        cost_estimate=STEP,
        name="last_sum",
    )(owners, *arrived, part, placed)[0]


def down_kernel(flags, own, owners, hidden, *rest):
    count = len(flags)
    weights, rest = rest[:count], rest[count:]
    terms, outs = rest[: sum(flags) + own], rest[sum(flags) + own :]
    taken = 0
    for i in range(count):
        total = jnp.dot(hidden[...], weights[i][...], preferred_element_type=F32)
        for term in terms[taken : taken + flags[i] + own]:
            total = total + term[...].astype(F32)
        taken += flags[i]
        outs[i][...] = total.astype(BF16)


def down(flags, owners, hidden, weights, arrived, own=()):
    m, cols = hidden.shape[0], weights[0].shape[1]
    return pl.pallas_call(
        functools.partial(down_kernel, flags, len(own)),
        out_shape=[jax.ShapeDtypeStruct((m, cols), BF16) for _ in flags],
        in_specs=[SMEM] + [VMEM] * (1 + len(flags) + len(arrived) + len(own)),
        out_specs=[VMEM] * len(flags),
        compiler_params=params(16),
        cost_estimate=STEP,
        name="down_sum",
    )(owners, hidden, *weights, *arrived, *own)


class Chain:
    def __init__(self, n, order, own, last):
        self.n, self.half, self.last = n, n // 2, last
        self.fw = [(order[i], order[(i + 1) % n]) for i in range(n)]
        self.bw = [(b, a) for a, b in self.fw]
        self.own, self.ahead, self.behind, self.hops = own, [own], [own], 0

    def done(self):
        return self.hops == self.half

    def parts(self):
        return [self.own] + self.ahead[1:] + self.behind[:0:-1]


def settle_kernel(*refs):
    for i in range(len(refs) // 2):
        refs[len(refs) // 2 + i][...] = refs[i][...]


def settle(*arrays):
    return pl.pallas_call(
        settle_kernel,
        out_shape=[jax.ShapeDtypeStruct(x.shape, x.dtype) for x in arrays],
        in_specs=[VMEM] * len(arrays),
        out_specs=[VMEM] * len(arrays),
        cost_estimate=STEP,
        name="settle",
    )(*arrays)


def tick_kernel(token, out):
    out[...] = token[...]


def tick(token):
    return pl.pallas_call(
        tick_kernel,
        out_shape=jax.ShapeDtypeStruct(token.shape, token.dtype),
        in_specs=[VMEM],
        out_specs=VMEM,
        cost_estimate=STEP,
        name="tick",
    )(token)


class Order:
    def __init__(self, ids):
        self.ids, self.last = ids, ()
        self.token = jnp.zeros((8, HD), F32)

    def after(self):
        return lax.optimization_barrier((self.ids, *self.last))[0]

    def mark(self, *out):
        self.last = out
        return out[0]

    def tick(self):
        self.token = tick(lax.optimization_barrier((self.token, *self.last))[0])

    def tied(self, *arrays):
        out = lax.optimization_barrier((*arrays, self.token, *self.last))
        self.last, self.token = (out[0],), out[len(arrays)]
        return out[: len(arrays)]

    def hop(self, chain):
        chain.hops += 1
        f, b = chain.ahead[-1], chain.behind[-1]
        f, b = self.tied(f, b)
        if chain.done() and chain.last == "fw":
            chain.ahead.append(lax.ppermute(f, "tok", chain.fw))
        elif chain.done():
            chain.behind.append(lax.ppermute(b, "tok", chain.bw))
        else:
            chain.ahead.append(lax.ppermute(f, "tok", chain.fw))
            chain.behind.append(lax.ppermute(b, "tok", chain.bw))


class Sum:
    def __init__(self, run, chain, hidden, blocks, own):
        self.run, self.chain, self.hidden, self.blocks = run, chain, hidden, blocks
        self.own, self.step, self.arrived = own, 0, ()

    def call(self, blocks, flags, own=()):
        weights = [self.blocks["down", -b % self.chain.n] for b in blocks]
        out = down(flags, self.run.after(), self.hidden, weights, self.arrived, own)
        self.run.mark(out[0])
        return out

    def hop(self):
        chain = self.chain
        d, forward = chain.half - self.step, chain.last == "fw"
        if self.step == 0:
            out = self.run.tied(*self.call([d], [0]))
            self.arrived = (lax.ppermute(out[0], "tok", chain.fw if forward else chain.bw),)
        else:
            flags = [1, 1] if self.step > 1 else ([1, 0] if forward else [0, 1])
            out = self.run.tied(*self.call([d, -d], flags))
            self.arrived = (lax.ppermute(out[0], "tok", chain.fw), lax.ppermute(out[1], "tok", chain.bw))
        self.step += 1

    def finish(self):
        return self.call([0], [2], (self.own,))[0]


def shards(
    pre_q,
    pre_kv,
    pre_segment,
    dec_q,
    cache,
    cache_len,
    slot_request,
    resid,
    wo,
    tenant,
    norm_gain,
    w_gate,
    w_up,
    w_down,
):
    n, groups = lax.axis_size("tok"), lax.axis_size("grp")
    tok, grp = lax.axis_index("tok"), lax.axis_index("grp")
    local = pre_q.shape[0]
    rows = local // 2
    cols = wo.shape[1]
    half = n // 2
    spare = -(-n // 16) * 16
    order = ring_order(n)
    ids = jnp.arange(n, dtype=jnp.int32)
    place = sum(jnp.where(tok == t, i, 0) for i, t in enumerate(order)).astype(jnp.int32)
    spots = (place - ids) % n
    owners = sum(jnp.where(spots == i, t, 0) for i, t in enumerate(order)).astype(jnp.int32)
    owners = jnp.concatenate([owners, jnp.reshape(grp, (1,)).astype(jnp.int32)])

    def split(a):
        a = a.reshape(n, local + 1, -1)
        first = a[:, :rows].reshape(n * rows, -1)
        second = a[:, rows:local].reshape(n * rows, -1)
        tail = jnp.pad(a[:, local], ((0, spare - n), (0, 0)))
        return first, jnp.concatenate([second, tail], axis=0)

    tenants = jnp.concatenate(split(tenant[0][:, None]), axis=0)
    run = Order(owners)

    def chain(own, last):
        return Chain(n, order, own, last)

    own_keys, own_values = pack(pre_kv, dec_q)
    keys, values = chain(own_keys, "fw"), chain(own_values, "bw")
    run.hop(keys)
    run.tick()
    run.hop(values)
    tenants, gain = settle(tenants, norm_gain)
    run.mark(*run.last, tenants, owners)
    while not keys.done():
        run.tick()
        run.hop(keys)
        run.tick()
        run.hop(values)
    choices = list(pick(n, groups, run.after(), slot_request, keys.parts()))
    run.mark(choices[0])
    for j in range(1, groups):
        (choices[j],) = run.tied(choices[j])
        choices[j] = lax.ppermute(choices[j], "grp", [(i, i ^ j) for i in range(groups)])
    kv = keys.parts() + values.parts()
    a = chain(run.mark(attention(0, rows, run.after(), pre_q, pre_segment, kv)), "fw")
    run.hop(a)
    dec = run.mark(decode(n, run.after(), slot_request, cache_len, choices, cache))
    b = chain(run.mark(attention(rows, rows, run.after(), pre_q, pre_segment, kv, (dec,))), "bw")
    run.hop(b)
    run.hop(a)
    weights = (w_gate, w_up, w_down)
    wide = w_gate.shape[1]
    far = [d for d in range(half - 1, half + 2)]
    fetches = [
        Fetch([0], [0]),
        Fetch([1, n - 1]),
        Fetch((), [1, n - 1]),
        Fetch([half], [half]),
    ]
    fetches.insert(0, Fetch((), (), far))
    store = {}

    def fetch_some():
        if fetches:
            fetch = fetches.pop(0)
            out = fetch_early(fetch, run.after(), weights, cols, wide)
            run.mark(out[0])
            fetch.keep(out, store)

    fetch_some()
    run.hop(b)
    fetch_some()
    while not a.done():
        run.hop(a)
        fetch_some()
        run.hop(b)
        fetch_some()
    while fetches:
        fetch_some()
    mixed_a = run.mark(project(rows, 0, 0, run.after(), a.parts(), wo, resid))
    g = chain(mixed_a, "fw")
    run.hop(g)
    mixed_b = run.mark(project(rows, spare, rows, run.after(), b.parts(), wo, resid))
    h = chain(mixed_b, "bw")
    run.hop(h)

    m_a, m = mixed_a.shape[0], tenants.shape[0]
    held = ()

    def add(lo, hi, shares, parts, fetch):
        w = [store["gate", tuple(shares)], store["up", tuple(shares)]]
        out = feed(lo, hi, shares, run.after(), tenants, gain, weights, w, parts, held, fetch)
        run.mark(out[2])
        fetch.keep(out[3:], store)
        return out[:3]

    def arrived(i):
        return [g.ahead[i], h.ahead[i], g.behind[i], h.behind[i]]

    def pair(i):
        return [i, n - i] if 1 < i < half else []

    def missing(ds):
        return [d for d in ds if ("down", d) not in store]

    held = add(0, m, [0], [mixed_a, mixed_b], Fetch(pair(2)))
    run.hop(g)
    run.hop(h)
    for i in range(1, half - 1):
        more = missing([half - 2, half + 2]) if i == half - 2 else []
        held = add(0, m, [i, n - i], arrived(i), Fetch(pair(i + 2), pair(i + 1), more))
        run.hop(g)
        run.hop(h)
    i = half - 1
    held = add(0, m_a, [i, n - i], arrived(i)[::2], Fetch((), (), missing(range(1, n))))

    last = [store["gate", (half,)], store["up", (half,)]]

    def finish(lo, hi, part):
        return run.mark(hide(lo, hi, half, run.after(), tenants, gain, last, part, held))

    hid_a = finish(0, m_a, g.ahead[half])
    sum_a = Sum(run, g, hid_a, store, mixed_a)
    sum_a.hop()
    held = add(m_a, m, [i, n - i], arrived(i)[1::2], Fetch((), (), [0]))
    hid_b = finish(m_a, m, h.behind[half])
    sum_b = Sum(run, h, hid_b, store, mixed_b)
    sum_b.hop()
    for _ in range(1, half):
        sum_a.hop()
        sum_b.hop()
    out_a, part_b = put_rows(
        n, rows, run.after(), hid_a, store["down", 0], sum_a.arrived, mixed_a, hid_b, mixed_b
    )
    run.mark(out_a)
    return assemble(n, rows, run.after(), sum_b.arrived, part_b, out_a)


def solution(mesh):
    in_specs = (
        P(("grp", "tok"), None),
        P(("grp", "tok"), None),
        P("grp", None),
        P(("grp", "tok"), None),
        P(("grp", "tok"), None, None),
        P(("grp", "tok")),
        P(),
        P("grp", "tok"),
        P(None, "tok"),
        P("grp", None),
        P(),
        P(None, "tok"),
        P(None, "tok"),
        P("tok", None),
    )
    out_specs = P("grp", "tok")
    return jax.shard_map(shards, mesh=mesh, in_specs=in_specs, out_specs=out_specs, check_vma=False)
```
